256 devices in a mesh: batch: 16 (over z, core), tm: 16 (over x, y).
Axes of the slice: x: 4, y: 4, z: 8, core: 2. Of those that a mesh axis runs over, the one named last changes fastest.
Arguments:
- feat_a: bfloat16 [16, 16, 4096, 256], P('batch', 'tm'), may hold values from -6 to 6
- feat_b: bfloat16 [16, 16, 4096, 256], P('batch', 'tm'), may hold values from -6 to 6
- flow_in_weight: float32 [128, 81], replicated, may hold values from -0.625 to 0.625
- flow_entry_bias: float32 [128], replicated, may hold values from -3 to 3
- flow_out_weight: float32 [3, 3, 2, 128], replicated, may hold values from -0.1875 to 0.1875
- frame_mix: float32 [16, 16], replicated, may hold values from -1.5 to 1.5
- expand_weight: bfloat16 [256, 1024], replicated, may hold values from -1.5 to 1.5
- expand_bias: float32 [1024], replicated, may hold values from -3 to 3
Outputs:
- flow: float32 [16, 16, 2, 4096], P('batch', 'tm')
- cov_grad: bfloat16 [2, 16, 16, 256, 1024], P(None, 'batch', None, 'tm')
The draws below stay inside these ranges and needn't reach their ends.
All inputs are finite; a program needn't handle non-finite values.
Results may differ from the reference program's by a relative error of at most 0.0061.
Values may be sent and summed in bfloat16 or wider, within the bound.
A program may use at most 192 MiB of HBM per device.

```python
import math
import jax
import jax.numpy as jnp
from jax import lax

HF = 64
WF = 64
D_FEAT = 256
EXP = 1024
DEC = 128
RADIUS = 4
FRAMES = 16
CLIPS = 16
POSITIONS = 4096
POOLED = 256
DISP = 81
ROWS = 65536


def steps_of(key, dims, cuts, smallest, top_value):
    gain = 1.0
    for axis_at, parts in cuts:
        steps = jax.random.uniform(jax.random.fold_in(jax.random.fold_in(key, 6), axis_at), (parts,), jnp.float32, smallest / len(cuts), top_value / len(cuts))
        gain = gain * jnp.repeat(jnp.exp(steps), dims[axis_at] // parts).reshape((-1,) + (1,) * (len(dims) - 1 - axis_at))
    return gain


def normal_values(key, dims, width, limit, pieces=(), kind=jnp.bfloat16):
    array = jax.random.normal(key, dims, jnp.float32) * width
    if len(pieces) > 0:
        array = steps_of(key, dims, pieces, -0.22, 0.18) * array
    return jnp.clip(array, min=-limit, max=limit).astype(kind)


def setup_inputs(seed: int = 0) -> dict:
    streams_of = jax.random.split(jax.random.key(seed), 9)
    return {
        "feat_a": normal_values(streams_of[0], (CLIPS, FRAMES, POSITIONS, D_FEAT), 1.0, 6.0, ((0, 16), (1, 16))),
        "feat_b": normal_values(streams_of[1], (CLIPS, FRAMES, POSITIONS, D_FEAT), 1.0, 6.0, ((0, 16), (1, 16))),
        "flow_in_weight": normal_values(streams_of[2], (DEC, DISP), DISP ** -0.5, 0.625, (), jnp.float32),
        "flow_entry_bias": normal_values(streams_of[3], (DEC,), 0.5, 3.0, (), jnp.float32),
        "flow_out_weight": normal_values(streams_of[4], (3, 3, 2, DEC), (9 * DEC) ** -0.5, 0.1875, (), jnp.float32),
        "frame_mix": normal_values(streams_of[5], (FRAMES, FRAMES), FRAMES ** -0.5, 1.5, (), jnp.float32),
        "expand_weight": normal_values(streams_of[6], (D_FEAT, EXP), (D_FEAT // 16) ** -0.5, 1.5),
        "expand_bias": normal_values(streams_of[7], (EXP,), 0.5, 3.0, (), jnp.float32),
    }


def volume(first, latter_item):
    span = 2 * RADIUS + 1
    left = first.astype(jnp.float32)
    border_filled = jnp.pad(latter_item.astype(jnp.float32), ((RADIUS, RADIUS), (RADIUS, RADIUS), (0, 0)))
    layers = []
    for row_shift in range(span):
        for col_shift in range(span):
            moved = border_filled[row_shift:row_shift + HF, col_shift:col_shift + WF]
            layers.append(lax.optimization_barrier(jnp.sum(left * moved, axis=-1)).reshape(-1))
    return jnp.stack(layers) / math.sqrt(D_FEAT)

def decode(corr, flow_in_weight, flow_entry_bias, flow_out_weight):
    top_precision = lax.Precision.HIGHEST
    hidden = jax.nn.gelu(jnp.dot(flow_in_weight, corr, precision=top_precision) + flow_entry_bias[:, None])
    border_filled = jnp.pad(hidden.reshape(DEC, HF, WF), ((0, 0), (1, 1), (1, 1)))
    output = jnp.zeros((2, HF * WF), jnp.float32)
    for row_tap in range(3):
        for column_offset in range(3):
            window = border_filled[:, row_tap:row_tap + HF, column_offset:column_offset + WF].reshape(DEC, HF * WF)
            output = output + jnp.dot(flow_out_weight[row_tap, column_offset], window, precision=top_precision)
    return output

def pool_view(feat):

    def one_clip(clip):
        blocks = clip.astype(jnp.float32).reshape(FRAMES, HF // 4, 4, WF // 4, 4, D_FEAT)
        return blocks.mean(axis=(2, 4)).reshape(FRAMES, POOLED, D_FEAT).astype(jnp.bfloat16)
    return lax.map(one_clip, feat)

def view_grad(feat, frame_mix, expand_weight, expand_bias):
    top_precision = lax.Precision.HIGHEST
    pooled = pool_view(feat)
    mixed = jnp.einsum('gf,cfqd->cgqd', frame_mix, pooled.astype(jnp.float32), precision=top_precision).astype(jnp.bfloat16)
    embed = jax.nn.gelu(jnp.dot(mixed.reshape(-1, D_FEAT), expand_weight, preferred_element_type=jnp.float32) + expand_bias).astype(jnp.bfloat16)
    values = embed.astype(jnp.float32)
    sums = lax.optimization_barrier(jnp.sum(values, axis=0))
    gram = jnp.dot(values.T, values, precision=top_precision)
    covariance_matrix = (gram - jnp.outer(sums, sums) / ROWS) / (ROWS - 1)
    covariance_matrix = covariance_matrix * (1.0 - jnp.eye(EXP, dtype=jnp.float32))
    grad = jnp.dot(values - sums / ROWS, covariance_matrix, precision=top_precision) / math.sqrt(EXP)
    return grad.astype(jnp.bfloat16).reshape(CLIPS, FRAMES, POOLED, EXP)

def reference(feat_a, feat_b, flow_in_weight, flow_entry_bias, flow_out_weight, frame_mix, expand_weight, expand_bias):
    following = jnp.concatenate([feat_a[:, 1:], jnp.zeros_like(feat_a[:, :1])], axis=1)
    firsts = feat_a.reshape(CLIPS * FRAMES, HF, WF, D_FEAT)
    seconds = following.reshape(CLIPS * FRAMES, HF, WF, D_FEAT)

    def one_pair(pair):
        corr = volume(pair[0], pair[1])
        return decode(corr, flow_in_weight, flow_entry_bias, flow_out_weight)
    flow = lax.map(one_pair, (firsts, seconds)).reshape(CLIPS, FRAMES, 2, POSITIONS)
    grad_a = view_grad(feat_a, frame_mix, expand_weight, expand_bias)
    grad_b = view_grad(feat_b, frame_mix, expand_weight, expand_bias)
    return (flow, jnp.stack([grad_a, grad_b]))
```

```python
import functools
import math

import jax
import jax.numpy as jnp
from jax import lax
from jax.experimental import pallas as pl
from jax.experimental.pallas import tpu as pltpu
from jax.sharding import PartitionSpec as P

MESH = pl.DeviceIdType.MESH
F32 = jnp.float32
BF16 = jnp.bfloat16

HF = 64
WF = 64
D_FEAT = 256
EXP = 1024
HALF = EXP // 2
DEC = 128
DISP = 81
POSITIONS = HF * WF
POOLED = 256
GROUP = 4 * WF
TASK = 32 * WF
REACH = 4 * WF
NEXT_ROWS = TASK + 2 * REACH
STRIP = 34 * WF

NN = (((1,), (0,)), ((), ()))
NT = (((1,), (1,)), ((), ()))
TN = (((0,), (0,)), ((), ()))


def mm(a, b, dims=NN, precision=None):
    return lax.dot_general(a, b, dims, precision=precision, preferred_element_type=F32)


def iota(shape, axis):
    return lax.broadcasted_iota(jnp.int32, shape, axis)


def gelu(x):
    return 0.5 * x * (1.0 + jnp.tanh(math.sqrt(2.0 / math.pi) * (x + 0.044715 * (x * x * x))))


def one_hot(condition):
    return jnp.where(condition, 1.0, 0.0).astype(BF16)


def band_weights(w_in, odd):
    shape = (5 * 128, DISP)
    row, col = iota(shape, 0), iota(shape, 1)
    lane = (row + 4) & 127
    dy = (row >> 7) * 2 + 1 - (lane >> 6) - odd
    dx = lane & 63
    hit = (dx < 9) & (dy >= 0) & (dy < 9) & (dy * 9 + dx == col)
    return (mm(one_hot(hit), w_in.astype(BF16), NT) * (1.0 / math.sqrt(D_FEAT))).astype(BF16)


def conv_weights(w_out_ref):
    zeros = jnp.zeros((2, DEC), F32)
    rows = []
    for kx in range(3):
        rows += [w_out_ref[ky, kx] for ky in range(3)] + [zeros]
    rows += [jnp.zeros((8, DEC), F32)]
    return jnp.concatenate(rows, axis=0).astype(BF16)


def mixing_weights(mix, frames, block):
    size = frames * block
    spread = one_hot(lax.div(iota((size, frames), 0), block) == iota((size, frames), 1))
    same = lax.rem(iota((size, size), 0), block) == lax.rem(iota((size, size), 1), block)
    high = mix.astype(BF16)
    low = (mix - high.astype(F32)).astype(BF16)
    parts = []
    for part in (high, low):
        rows = mm(spread, part).astype(BF16)
        parts.append(jnp.where(same, mm(rows, spread, NT), 0.0).astype(BF16))
    return parts


def hidden_rows(first_ref, first_at, next_ref, next_at, band_ref, bias, hid_ref):
    x, lane = 63 - iota((WF, 128), 0), (iota((WF, 128), 1) + 4) & 63
    inside = (lane < 9) & (x + lane >= 4) & (x + lane < WF + 4)
    row, col = iota((GROUP, GROUP), 0), iota((GROUP, GROUP), 1)
    turn = one_hot((row ^ 63) == col)

    def group(g, carry):
        at = pl.multiple_of(g * GROUP, GROUP)
        first = first_ref[pl.ds(first_at + at, GROUP), :]
        latter = next_ref[pl.ds(next_at + at, 3 * GROUP), :]
        products = mm(mm(turn, first).astype(BF16), latter, NT)
        for odd in range(2):
            pieces = []
            for i in (odd, odd + 2):
                blocks = []
                for m in range(i // 2, i // 2 + 5):
                    block = products[i * WF : (i + 1) * WF, m * 128 : (m + 1) * 128]
                    block = pltpu.roll(block, 1, 1, stride=1, stride_axis=0)
                    blocks.append(jnp.where(inside, block, 0.0).astype(BF16))
                pieces.append(jnp.concatenate(blocks, axis=1))
            skewed = jnp.concatenate(pieces, axis=0)
            hidden = gelu(mm(skewed, band_ref[odd]) + bias).astype(BF16)
            hidden = mm(turn[:128, :128], hidden).astype(BF16)
            hid_ref[pl.ds(at + odd * WF, WF), :] = hidden[:WF]
            hid_ref[pl.ds(at + (odd + 2) * WF, WF), :] = hidden[WF:]
        return carry

    lax.fori_loop(0, TASK // GROUP, group, 0)


def flow_rows(hid_ref, conv, base):
    taps = mm(conv, hid_ref[...], NT)
    lane = iota((8, TASK), 1) & 63
    across = (
        taps[8:16]
        + jnp.where(lane != 0, pltpu.roll(taps[0:8], 1, 1), 0.0)
        + jnp.where(lane != 63, pltpu.roll(taps[16:24], TASK - 1, 1), 0.0)
    )
    wide = TASK + 256
    across = jnp.concatenate([across, jnp.zeros((8, 256), F32)], axis=1)
    total = pltpu.roll(across, base + 64, 1)
    middle = pltpu.roll(across, base, 1) if base else across
    total = total + pltpu.roll(middle, 6, 0)
    total = total + pltpu.roll(pltpu.roll(across, (base + wide - 64) % wide, 1), 4, 0)
    return total[:, :STRIP]


def kernel(
    nx,
    nz,
    fa_ref,
    fb_ref,
    w_in_ref,
    b_in_ref,
    w_out_ref,
    mix_ref,
    ew_ref,
    eb_ref,
    flow_ref,
    grad_ref,
    a_buf,
    b_buf,
    rn_buf,
    rp_buf,
    band,
    conv,
    mixer,
    pooled,
    got1,
    got2,
    z_buf,
    zc_buf,
    zt_buf,
    mean0,
    mean_x,
    mean_y,
    mean1,
    mean_x2,
    mean_y2,
    mean2,
    mean_z,
    dev,
    send_1,
    recv_1,
    send_2,
    recv_2,
    send_3,
    recv_3,
    small,
    cov_z,
    cov_mid,
    cov_all,
    matrix,
    hid,
    strip_send,
    strip_recv,
    strip_own,
    grads,
    local_sem,
    send_sem,
    recv_sem,
):
    frames = nx * nx
    block = POOLED // frames
    rows = frames * block
    local_rows = 2 * rows
    lb = HALF // nx
    zr = lb // nz

    batch, t = lax.axis_index("batch"), lax.axis_index("tm")
    z, core = lax.div(batch, 2), lax.rem(batch, 2)
    x, y = lax.div(t, nx), lax.rem(t, nx)
    other = 1 - core

    def around(i, d, n):
        return lax.rem(i + d, n)

    x_peers = [(batch, around(x, d, nx) * nx + y) for d in range(1, nx)]
    y_peers = [(batch, x * nx + around(y, d, nx)) for d in range(1, nx)]
    z_peers = [(around(z, d, nz) * 2 + core, t) for d in range(1, nz)]
    partner = (z * 2 + other, t)
    y_partners = [(z * 2 + other, x * nx + around(y, d, nx)) for d in range(1, nx)]
    before = (batch, lax.rem(t + frames - 1, frames))
    after = (batch, lax.rem(t + 1, frames))

    count = [0]

    def remote(src, dst, device):
        i = count[0]
        count[0] += 1
        return pltpu.make_async_remote_copy(
            src_ref=src,
            dst_ref=dst,
            send_sem=send_sem.at[i],
            recv_sem=recv_sem.at[i],
            device_id=device,
            device_id_type=MESH,
        )

    def start(copies):
        for copy in copies:
            copy.start()
        started.extend(copies)

    def arrived(copies):
        for copy in copies:
            copy.wait_recv()

    started = []

    barrier = pltpu.get_barrier_semaphore()
    everyone = x_peers + y_peers + z_peers + [partner] + y_partners + [before, after]
    for device in everyone:
        pl.semaphore_signal(barrier, inc=1, device_id=device, device_id_type=MESH)

    load_a = pltpu.make_async_copy(fa_ref.at[0, 0], a_buf.at[pl.ds(REACH, POSITIONS)], local_sem.at[0])
    load_b = pltpu.make_async_copy(fb_ref.at[0, 0], b_buf, local_sem.at[1])
    load_a.start()
    load_b.start()

    a_buf[pl.ds(0, REACH), :] = jnp.zeros((REACH, D_FEAT), BF16)
    rn_buf[pl.ds(TASK + REACH, REACH), :] = jnp.zeros((REACH, D_FEAT), BF16)

    @pl.when(t == frames - 1)
    def _():
        rn_buf[pl.ds(0, TASK + REACH), :] = jnp.zeros((TASK + REACH, D_FEAT), BF16)

    @pl.when(t == 0)
    def _():
        rp_buf[...] = jnp.zeros((TASK, D_FEAT), BF16)

    mixer[0], mixer[1] = mixing_weights(mix_ref[...], frames, block)

    span = POSITIONS // frames
    prow, pcol = iota((block, span), 0), iota((block, span), 1)
    pooled_at = lax.div(pcol, GROUP) * 16 + lax.div(pcol & 63, 4)
    pool = one_hot(pooled_at == prow)
    load_a.wait()
    load_b.wait()

    def pool_block(k, carry):
        kx, ky = lax.div(k, nx), lax.rem(k, nx)
        at = pl.multiple_of(k * span, span)
        from_a = mm(pool, a_buf[pl.ds(REACH + at, span), :]) * (1.0 / 16.0)
        pooled[kx, ky, 0] = from_a.astype(BF16)
        from_b = mm(pool, b_buf[pl.ds(at, span), :]) * (1.0 / 16.0)
        pooled[kx, ky, 1] = from_b.astype(BF16)
        return carry

    lax.fori_loop(0, frames, pool_block, 0)
    pl.semaphore_wait(barrier, len(everyone))

    stage = [
        remote(pooled.at[around(x, d, nx)], got1.at[x], x_peers[d - 1]) for d in range(1, nx)
    ]
    start(stage)

    to_before = remote(
        a_buf.at[pl.ds(REACH + TASK - REACH, TASK + REACH)], rn_buf.at[pl.ds(0, TASK + REACH)], before
    )
    to_after = remote(a_buf.at[pl.ds(REACH, TASK)], rp_buf, after)

    @pl.when(t > 0)
    def _():
        to_before.start()

    @pl.when(t < frames - 1)
    def _():
        to_after.start()

    got1[x] = pooled[x]
    arrived(stage)
    stage = []
    for d in range(nx):
        for flip in range(2):
            if d == 0 and flip == 0:
                continue
            view = other if flip else core
            source = got1.at[:, around(y, d, nx), view]
            target = partner if d == 0 else (y_partners if flip else y_peers)[d - 1]
            stage.append(remote(source, got2.at[core, :, y], target))
    start(stage)
    got2[core, :, y] = got1[:, y, core]
    band[0] = band_weights(w_in_ref[...], 0)
    band[1] = band_weights(w_in_ref[...], 1)
    conv[...] = conv_weights(w_out_ref)
    arrived(stage)

    total = [jnp.zeros((1, 256), F32) for _ in range(EXP // 256)]
    for clip in range(2):
        features = got2[clip].reshape(rows, D_FEAT)
        mixed = (mm(mixer[0], features) + mm(mixer[1], features)).astype(BF16)
        for k in range(EXP // 256):
            cols = pl.ds(k * 256, 256)
            value = gelu(mm(mixed, ew_ref[:, cols]) + eb_ref[:, cols]).astype(BF16)
            z_buf[pl.ds(clip * rows, rows), cols] = value
            total[k] = total[k] + jnp.sum(value.astype(F32), axis=0, keepdims=True)
    mean = jnp.concatenate(total, axis=1) / local_rows
    mean0[0] = mean
    share_x = [remote(mean0.at[0], mean_x.at[d - 1], x_peers[d - 1]) for d in range(1, nx)]
    share_y = [remote(mean0.at[0], mean_y.at[d - 1], y_peers[d - 1]) for d in range(1, nx)]
    start(share_x)
    start(share_y)

    def center(k, carry):
        part = pl.ds(pl.multiple_of(k * 64, 64), 64)
        zc_buf[part, :] = (z_buf[part, :].astype(F32) - mean).astype(BF16)
        return carry

    lax.fori_loop(0, local_rows // 64, center, 0)
    for k in range(EXP // 256):
        zt_buf[pl.ds(k * 256, 256), :] = zc_buf[:, pl.ds(k * 256, 256)].T
    left, right = pl.ds(0, HALF), pl.ds(HALF, HALF)

    for k in range(HALF // 256):
        cols = pl.ds(HALF + k * 256, 256)
        cross = mm(zt_buf[left, :], zc_buf[:, cols]).astype(BF16)
        for j in range(256 // lb):
            send_1[0, k * (256 // lb) + j] = cross[:, j * lb : (j + 1) * lb]
    first_x = [
        remote(send_1.at[0, around(x, d, nx)], recv_1.at[0, d - 1], x_peers[d - 1])
        for d in range(1, nx)
    ]
    start(first_x)
    row_at, col_at = iota((HALF, 256), 0), iota((HALF, 256), 1)
    for k in range(HALF // 256):
        in_left = mm(zt_buf[left, :], zc_buf[:, pl.ds(k * 256, 256)])
        in_right = mm(zt_buf[right, :], zc_buf[:, pl.ds(HALF + k * 256, 256)])
        ahead = col_at + k * 256 - row_at
        both = jnp.where(ahead > 0, in_left, jnp.where(ahead < 0, in_right, 0.0)).astype(BF16)
        for j in range(256 // lb):
            send_1[1, k * (256 // lb) + j] = both[:, j * lb : (j + 1) * lb]
    first_y = [
        remote(send_1.at[1, around(y, d, nx)], recv_1.at[1, d - 1], y_peers[d - 1])
        for d in range(1, nx)
    ]
    start(first_y)

    def combine(own, parts, n):
        center = own
        for i in range(n - 1):
            center = center + parts[i]
        center = center / n
        lines = [own - center] + [parts[i] - center for i in range(n - 1)]
        lines += [jnp.zeros_like(own)] * (8 - n)
        dev[...] = jnp.concatenate(lines, axis=0)
        return center

    def outer(first_at, height, second_at):
        return mm(
            dev[:, pl.ds(first_at, height)],
            dev[:, pl.ds(second_at, lb)],
            TN,
            precision=lax.Precision.HIGHEST,
        )

    def triangles(first_at, height, block_at, inner_at):
        in_left = outer(first_at, height, block_at)
        in_right = outer(HALF + first_at, height, HALF + block_at)
        ahead = (block_at + iota((height, lb), 1)) - (inner_at + iota((height, lb), 0))
        return jnp.where(ahead > 0, in_left, jnp.where(ahead < 0, in_right, 0.0))

    x_at, y_at = pl.multiple_of(x * lb, lb), pl.multiple_of(y * lb, lb)

    arrived(share_x)
    center_x = combine(mean0[0], mean_x, nx)
    mean1[0] = center_x
    carry_x = [remote(mean1.at[0], mean_x2.at[d - 1], y_peers[d - 1]) for d in range(1, nx)]
    start(carry_x)
    part = local_rows * outer(0, HALF, HALF + x_at)
    arrived(first_x)
    part = part + send_1[0, x].astype(F32)
    for i in range(nx - 1):
        part = part + recv_1[0, i].astype(F32)
    send_2[0] = part.astype(BF16)
    second_x = [
        remote(
            send_2.at[0, pl.ds(pl.multiple_of(around(y, d, nx) * lb, lb), lb)],
            recv_2.at[0, d - 1],
            y_peers[d - 1],
        )
        for d in range(1, nx)
    ]
    start(second_x)

    arrived(share_y)
    center_y = combine(mean0[0], mean_y, nx)
    mean1[1] = center_y
    carry_y = [remote(mean1.at[1], mean_y2.at[d - 1], x_peers[d - 1]) for d in range(1, nx)]
    start(carry_y)
    part = local_rows * triangles(0, HALF, y_at, 0)
    arrived(first_y)
    part = part + send_1[1, y].astype(F32)
    for i in range(nx - 1):
        part = part + recv_1[1, i].astype(F32)
    send_2[1] = part.astype(BF16)
    second_y = [
        remote(
            send_2.at[1, pl.ds(pl.multiple_of(around(x, d, nx) * lb, lb), lb)],
            recv_2.at[1, d - 1],
            x_peers[d - 1],
        )
        for d in range(1, nx)
    ]
    start(second_y)

    arrived(carry_x)
    center_xy = combine(mean1[0], mean_x2, nx)
    mean2[0] = center_xy
    carry_z = [remote(mean2.at[0], mean_z.at[d - 1], z_peers[d - 1]) for d in range(1, nz)]
    start(carry_z)
    part = (local_rows * nx) * outer(y_at, lb, HALF + x_at)
    arrived(second_x)
    part = part + send_2[0, pl.ds(y_at, lb)].astype(F32)
    for i in range(nx - 1):
        part = part + recv_2[0, i].astype(F32)
    send_3[0] = part.astype(BF16)

    arrived(carry_y)
    combine(mean1[1], mean_y2, nx)
    part = (local_rows * nx) * triangles(x_at, lb, y_at, x_at)
    arrived(second_y)
    part = part + send_2[1, pl.ds(x_at, lb)].astype(F32)
    for i in range(nx - 1):
        part = part + recv_2[1, i].astype(F32)
    send_3[1] = part.astype(BF16)

    def z_rows(i):
        return pl.ds(pl.multiple_of(i * zr, zr), zr)

    third = [
        remote(send_3.at[:, z_rows(around(z, d, nz))], recv_3.at[d - 1], z_peers[d - 1])
        for d in range(1, nz)
    ]
    start(third)
    arrived(carry_z)
    mean = combine(mean2[0], mean_z, nz)
    group_rows = local_rows * frames
    small[0] = group_rows * outer(y_at, lb, HALF + x_at)
    small[1] = group_rows * triangles(x_at, lb, y_at, x_at)
    arrived(third)
    part = small[:, z_rows(z), :] + send_3[:, z_rows(z), :].astype(F32)
    for i in range(nz - 1):
        part = part + recv_3[i].astype(F32)
    scale = 1.0 / (group_rows * nz - 1) / math.sqrt(EXP)
    cov_z[:, z_rows(z), :] = (part * scale).astype(BF16)

    back_z = [
        remote(cov_z.at[:, z_rows(z)], cov_z.at[:, z_rows(z)], z_peers[d - 1])
        for d in range(1, nz)
    ]
    start(back_z)

    def center_all(k, carry):
        part = pl.ds(pl.multiple_of(k * 64, 64), 64)
        zc_buf[part, :] = (z_buf[part, :].astype(F32) - mean).astype(BF16)
        return carry

    lax.fori_loop(0, local_rows // 64, center_all, 0)
    arrived(back_z)
    y_rows, x_rows = pl.ds(y_at, lb), pl.ds(x_at, lb)
    back_2 = [
        remote(cov_z.at[0], cov_mid.at[0, y_rows], y_peers[d - 1]) for d in range(1, nx)
    ] + [remote(cov_z.at[1], cov_mid.at[1, x_rows], x_peers[d - 1]) for d in range(1, nx)]
    start(back_2)
    cov_mid[0, y_rows] = cov_z[0]
    cov_mid[1, x_rows] = cov_z[1]
    arrived(back_2)
    back_1 = [
        remote(cov_mid.at[0], cov_all.at[0, x], x_peers[d - 1]) for d in range(1, nx)
    ] + [remote(cov_mid.at[1], cov_all.at[1, y], y_peers[d - 1]) for d in range(1, nx)]
    start(back_1)
    cov_all[0, x] = cov_mid[0]
    cov_all[1, y] = cov_mid[1]

    bias = b_in_ref[...]

    @pl.when(t > 0)
    def _():
        to_after.wait_recv()

    hidden_rows(rp_buf, 0, a_buf, 0, band, bias, hid)
    strip_send[...] = flow_rows(hid, conv[...], 0)
    strip = remote(strip_send, strip_recv, before)
    start([strip])

    @pl.when(t < frames - 1)
    def _():
        to_before.wait_recv()

    hidden_rows(a_buf, REACH + TASK, rn_buf, 0, band, bias, hid)
    strip_own[...] = flow_rows(hid, conv[...], 128)

    arrived(back_1)
    pieces = HALF // lb
    cross = jnp.concatenate([cov_all[0, k] for k in range(pieces)], axis=1)
    both = jnp.concatenate([cov_all[1, k] for k in range(pieces)], axis=1)
    turned = both.T
    ahead = iota((HALF, HALF), 1) - iota((HALF, HALF), 0)
    matrix[left, right] = cross
    matrix[right, left] = cross.T
    matrix[left, left] = jnp.where(ahead > 0, both, turned)
    matrix[right, right] = jnp.where(ahead < 0, both, turned)

    def gradient(slot, clip):
        lines = pl.ds(pl.multiple_of(clip * rows, rows), rows)
        for k in range(EXP // 256):
            cols = pl.ds(k * 256, 256)
            grads[slot, :, cols] = mm(zc_buf[lines, :], matrix[:, cols]).astype(BF16)

    gradient(0, other)
    hand_over = remote(grads.at[0], grad_ref.at[core], partner)
    start([hand_over])
    gradient(1, core)
    keep = pltpu.make_async_copy(grads.at[1], grad_ref.at[core], local_sem.at[2])
    keep.start()

    arrived([strip])
    edge = STRIP - 256
    top, bottom = strip_recv[...], strip_own[...]
    flow_ref[:, 0:edge] = top[0:2, :edge]
    flow_ref[:, edge:STRIP] = top[0:2, edge:] + bottom[0:2, :256]
    flow_ref[:, STRIP:] = bottom[0:2, 256:]

    arrived([hand_over])
    keep.wait()

    @pl.when(t > 0)
    def _():
        to_before.wait_send()

    @pl.when(t < frames - 1)
    def _():
        to_after.wait_send()

    for copy in started:
        copy.wait_send()


def on_device(
    nx,
    nz,
    feat_a,
    feat_b,
    flow_in_weight,
    flow_entry_bias,
    flow_out_weight,
    frame_mix,
    expand_weight,
    expand_bias,
):
    frames = nx * nx
    block = POOLED // frames
    rows = frames * block
    lb = HALF // nx
    zr = lb // nz
    copies = 15 * (nx - 1) + 2 + nz * 3 + 8 + nx * 6
    vmem = pl.BlockSpec(memory_space=pltpu.VMEM)
    hbm = pl.BlockSpec(memory_space=pl.ANY)
    scratch = [
        pltpu.VMEM((REACH + POSITIONS, D_FEAT), BF16),
        pltpu.VMEM((POSITIONS, D_FEAT), BF16),
        pltpu.VMEM((NEXT_ROWS, D_FEAT), BF16),
        pltpu.VMEM((TASK, D_FEAT), BF16),
        pltpu.VMEM((2, 640, DEC), BF16),
        pltpu.VMEM((32, DEC), BF16),
        pltpu.VMEM((2, rows, rows), BF16),
        pltpu.VMEM((nx, nx, 2, block, D_FEAT), BF16),
        pltpu.VMEM((nx, nx, 2, block, D_FEAT), BF16),
        pltpu.VMEM((2, nx, nx, block, D_FEAT), BF16),
        pltpu.VMEM((2 * rows, EXP), BF16),
        pltpu.VMEM((2 * rows, EXP), BF16),
        pltpu.VMEM((EXP, 2 * rows), BF16),
        pltpu.VMEM((1, 1, EXP), F32),
        pltpu.VMEM((nx - 1, 1, EXP), F32),
        pltpu.VMEM((nx - 1, 1, EXP), F32),
        pltpu.VMEM((2, 1, EXP), F32),
        pltpu.VMEM((nx - 1, 1, EXP), F32),
        pltpu.VMEM((nx - 1, 1, EXP), F32),
        pltpu.VMEM((1, 1, EXP), F32),
        pltpu.VMEM((nz - 1, 1, EXP), F32),
        pltpu.VMEM((8, EXP), F32),
        pltpu.VMEM((2, nx, HALF, lb), BF16),
        pltpu.VMEM((2, nx - 1, HALF, lb), BF16),
        pltpu.VMEM((2, HALF, lb), BF16),
        pltpu.VMEM((2, nx - 1, lb, lb), BF16),
        pltpu.VMEM((2, lb, lb), BF16),
        pltpu.VMEM((nz - 1, 2, zr, lb), BF16),
        pltpu.VMEM((2, lb, lb), F32),
        pltpu.VMEM((2, lb, lb), BF16),
        pltpu.VMEM((2, HALF, lb), BF16),
        pltpu.VMEM((2, nx, HALF, lb), BF16),
        pltpu.VMEM((EXP, EXP), BF16),
        pltpu.VMEM((TASK, DEC), BF16),
        pltpu.VMEM((8, STRIP), F32),
        pltpu.VMEM((8, STRIP), F32),
        pltpu.VMEM((8, STRIP), F32),
        pltpu.VMEM((2, rows, EXP), BF16),
        pltpu.SemaphoreType.DMA((3,)),
        pltpu.SemaphoreType.DMA((copies,)),
        pltpu.SemaphoreType.DMA((copies,)),
    ]
    flow, grads = pl.pallas_call(
        functools.partial(kernel, nx, nz),
        out_shape=[
            jax.ShapeDtypeStruct((2, POSITIONS), F32),
            jax.ShapeDtypeStruct((2, rows, EXP), BF16),
        ],
        in_specs=[hbm, hbm] + [vmem] * 6,
        out_specs=[vmem, hbm],
        scratch_shapes=scratch,
        compiler_params=pltpu.CompilerParams(
            collective_id=0, has_side_effects=True, vmem_limit_bytes=56 * 1024 * 1024
        ),
    )(
        feat_a,
        feat_b,
        flow_in_weight,
        flow_entry_bias.reshape(1, DEC),
        flow_out_weight,
        frame_mix,
        expand_weight,
        expand_bias.reshape(1, EXP),
    )
    return (
        flow.reshape(1, 1, 2, POSITIONS),
        grads.reshape(2, 1, frames, block, EXP),
    )


def solution(mesh):
    nx = math.isqrt(mesh.shape["tm"])
    nz = mesh.shape["batch"] // 2
    return jax.shard_map(
        functools.partial(on_device, nx, nz),
        mesh=mesh,
        in_specs=(
            P("batch", "tm", None, None),
            P("batch", "tm", None, None),
            P(),
            P(),
            P(),
            P(),
            P(),
            P(),
        ),
        out_specs=(P("batch", "tm", None, None), P(None, "batch", None, "tm", None)),
        check_vma=False,
    )
```

```python
import functools
import math

import jax
import jax.numpy as jnp
from jax import lax
from jax.experimental import pallas as pl
from jax.experimental.pallas import tpu as pltpu
from jax.sharding import PartitionSpec as P

MESH = pl.DeviceIdType.MESH
F32 = jnp.float32
BF16 = jnp.bfloat16

HF = 64
WF = 64
D_FEAT = 256
EXP = 1024
HALF = EXP // 2
DEC = 128
DISP = 81
POSITIONS = HF * WF
POOLED = 256
GROUP = 4 * WF
TASK = 32 * WF
REACH = 4 * WF
NEXT_ROWS = TASK + 2 * REACH
UNROLL = 2
STRIP = 34 * WF

SCHEDULE = {
    "exchange": [("send", 0, 1)],
    "embed": [("send", 1, 2)],
    "first": [("upper", 0, 2), ("lower", 0, 1)],
    "second": [("send", 2, 3), ("upper", 2, 4)],
    "third": [("send", 3, 4), ("lower", 1, 3)],
    "back z": [("upper", 4, 6)],
    "back 2": [("lower", 3, 5)],
    "back 1": [("upper", 6, 8), ("lower", 5, 8)],
}

NN = (((1,), (0,)), ((), ()))
NT = (((1,), (1,)), ((), ()))
TN = (((0,), (0,)), ((), ()))


def mm(a, b, dims=NN, precision=None):
    return lax.dot_general(a, b, dims, precision=precision, preferred_element_type=F32)


def iota(shape, axis):
    return lax.broadcasted_iota(jnp.int32, shape, axis)


def gelu(x):
    return 0.5 * x * (1.0 + jnp.tanh(math.sqrt(2.0 / math.pi) * (x + 0.044715 * (x * x * x))))


def one_hot(condition):
    return jnp.where(condition, 1.0, 0.0).astype(BF16)


def turn(size, kind):
    hit = (iota((size, size), 0) ^ 63) == iota((size, size), 1)
    return jnp.where(hit, 1.0, 0.0).astype(kind)


def band_weights(w_in, odd):
    shape = (5 * 128, DISP)
    row, col = iota(shape, 0), iota(shape, 1)
    lane = (row + 4) & 127
    dy = (row >> 7) * 2 + 1 - (lane >> 6) - odd
    dx = lane & 63
    hit = (dx < 9) & (dy >= 0) & (dy < 9) & (dy * 9 + dx == col)
    return (mm(one_hot(hit), w_in.astype(BF16)) * (1.0 / math.sqrt(D_FEAT))).astype(BF16)


def conv_weights(w_out_ref):
    zeros = jnp.zeros((2, DEC), F32)
    rows = []
    for kx in (2, 1, 0):
        rows += [w_out_ref[ky, kx] for ky in range(3)] + [zeros]
    rows += [jnp.zeros((8, DEC), F32)]
    return jnp.concatenate(rows, axis=0).astype(BF16)


def mixing_weights(mix, frames, block):
    size = frames * block
    spread = one_hot(lax.div(iota((size, frames), 0), block) == iota((size, frames), 1))
    same = lax.rem(iota((size, size), 0), block) == lax.rem(iota((size, size), 1), block)
    high = mix.astype(BF16)
    low = (mix - high.astype(F32)).astype(BF16)
    parts = []
    for part in (high, low):
        rows = mm(spread, part).astype(BF16)
        parts.append(jnp.where(same, mm(rows, spread, NT), 0.0).astype(BF16))
    return parts


def hidden_rows(low, high, first_ref, first_at, next_ref, next_at, band_ref, bias, hid_ref):
    x, lane = 63 - iota((WF, 128), 0), (iota((WF, 128), 1) + 4) & 63
    inside = (lane < 9) & (x + lane >= 4) & (x + lane < WF + 4)

    def group(g, carry):
        at = pl.multiple_of(g * GROUP, GROUP)
        first = first_ref[pl.ds(first_at + at, GROUP), :]
        latter = next_ref[pl.ds(next_at + at, 3 * GROUP), :]
        products = mm(first, latter, NT)
        for odd in range(2):
            pieces = []
            for i in (odd, odd + 2):
                blocks = []
                for m in range(i // 2, i // 2 + 5):
                    block = products[i * WF : (i + 1) * WF, m * 128 : (m + 1) * 128]
                    block = pltpu.roll(block, 1, 1, stride=1, stride_axis=0)
                    blocks.append(jnp.where(inside, block, 0.0).astype(BF16))
                pieces.append(jnp.concatenate(blocks, axis=1))
            skewed = jnp.concatenate(pieces, axis=0)
            hidden = gelu(mm(skewed, band_ref[odd]) + bias).astype(BF16)
            hid_ref[pl.ds(at + odd * WF, WF), :] = hidden[:WF]
            hid_ref[pl.ds(at + (odd + 2) * WF, WF), :] = hidden[WF:]
        return carry

    lax.fori_loop(low, high, group, 0, unroll=UNROLL)


def flow_rows(hid_ref, conv, base):
    taps = mm(conv, hid_ref[...], NT)
    lane = iota((8, TASK), 1) & 63
    across = (
        taps[8:16]
        + jnp.where(lane != 0, pltpu.roll(taps[0:8], 1, 1), 0.0)
        + jnp.where(lane != 63, pltpu.roll(taps[16:24], TASK - 1, 1), 0.0)
    )
    wide = TASK + 256
    across = jnp.concatenate([across, jnp.zeros((8, 256), F32)], axis=1)
    total = pltpu.roll(across, base + 64, 1)
    middle = pltpu.roll(across, base, 1) if base else across
    total = total + pltpu.roll(middle, 6, 0)
    total = total + pltpu.roll(pltpu.roll(across, (base + wide - 64) % wide, 1), 4, 0)
    blocks = [total[:, k * 128 : (k + 1) * 128] for k in range(STRIP // 128)]
    turned = mm(jnp.concatenate(blocks, axis=0), turn(128, F32), precision=lax.Precision.HIGHEST)
    return jnp.concatenate([turned[k * 8 : (k + 1) * 8] for k in range(STRIP // 128)], axis=1)


def kernel(
    nx,
    nz,
    fa_ref,
    fb_ref,
    w_in_ref,
    b_in_ref,
    w_out_ref,
    mix_ref,
    ew_ref,
    eb_ref,
    flow_ref,
    grad_ref,
    a_buf,
    b_buf,
    t_buf,
    rn_buf,
    rp_buf,
    band,
    conv,
    mixer,
    pooled,
    got1,
    got,
    z_buf,
    zc_buf,
    zt_buf,
    mean0,
    mean_x,
    mean_y,
    mean1,
    mean_x2,
    mean_y2,
    mean2,
    mean_z,
    dev,
    send_1,
    recv_1,
    send_2,
    recv_2,
    send_3,
    recv_3,
    small,
    cov_z,
    cov_mid,
    cov_all,
    matrix,
    hid,
    strip_send,
    strip_recv,
    strip_own,
    grads,
    local_sem,
    send_sem,
    recv_sem,
):
    frames = nx * nx
    block = POOLED // frames
    rows = frames * block
    local_rows = 2 * rows
    lb = HALF // nx
    zr = lb // nz

    batch, t = lax.axis_index("batch"), lax.axis_index("tm")
    z, core = lax.div(batch, 2), lax.rem(batch, 2)
    x, y = lax.div(t, nx), lax.rem(t, nx)
    other = 1 - core

    def around(i, d, n):
        return lax.rem(i + d, n)

    x_peers = [(batch, around(x, d, nx) * nx + y) for d in range(1, nx)]
    y_peers = [(batch, x * nx + around(y, d, nx)) for d in range(1, nx)]
    z_peers = [(around(z, d, nz) * 2 + core, t) for d in range(1, nz)]
    partner = (z * 2 + other, t)
    y_partners = [(z * 2 + other, x * nx + around(y, d, nx)) for d in range(1, nx)]
    before = (batch, lax.rem(t + frames - 1, frames))
    after = (batch, lax.rem(t + 1, frames))

    count = [0]

    def remote(src, dst, device):
        i = count[0]
        count[0] += 1
        return pltpu.make_async_remote_copy(
            src_ref=src,
            dst_ref=dst,
            send_sem=send_sem.at[i],
            recv_sem=recv_sem.at[i],
            device_id=device,
            device_id_type=MESH,
        )

    def start(copies):
        for copy in copies:
            copy.start()
        started.extend(copies)

    def arrived(copies):
        for copy in copies:
            copy.wait_recv()

    started = []

    barrier = pltpu.get_barrier_semaphore()
    everyone = x_peers + y_peers + z_peers + [partner] + y_partners + [before, after]
    for device in everyone:
        pl.semaphore_signal(barrier, inc=1, device_id=device, device_id_type=MESH)

    load_a = pltpu.make_async_copy(fa_ref.at[0, 0], a_buf.at[pl.ds(REACH, POSITIONS)], local_sem.at[0])
    load_b = pltpu.make_async_copy(fb_ref.at[0, 0], b_buf, local_sem.at[1])
    load_a.start()
    load_b.start()

    a_buf[pl.ds(0, REACH), :] = jnp.zeros((REACH, D_FEAT), BF16)
    rn_buf[pl.ds(TASK + REACH, REACH), :] = jnp.zeros((REACH, D_FEAT), BF16)

    @pl.when(t == frames - 1)
    def _():
        rn_buf[pl.ds(0, TASK + REACH), :] = jnp.zeros((TASK + REACH, D_FEAT), BF16)

    @pl.when(t == 0)
    def _():
        rp_buf[...] = jnp.zeros((TASK, D_FEAT), BF16)

    mixer[0], mixer[1] = mixing_weights(mix_ref[...], frames, block)

    span = POSITIONS // frames
    prow, pcol = iota((block, span), 0), iota((block, span), 1)
    pooled_at = lax.div(pcol, GROUP) * 16 + lax.div(pcol & 63, 4)
    pool = one_hot(pooled_at == prow)
    load_a.wait()
    load_b.wait()

    def pool_block(k, carry):
        kx, ky = lax.div(k, nx), lax.rem(k, nx)
        at = pl.multiple_of(k * span, span)
        from_a = mm(pool, a_buf[pl.ds(REACH + at, span), :]) * (1.0 / 16.0)
        pooled[kx, ky, 0] = from_a.astype(BF16)
        from_b = mm(pool, b_buf[pl.ds(at, span), :]) * (1.0 / 16.0)
        pooled[kx, ky, 1] = from_b.astype(BF16)
        return carry

    lax.fori_loop(0, frames, pool_block, 0)
    pl.semaphore_wait(barrier, len(everyone))

    exchange = [
        remote(pooled.at[around(x, d, nx)], got1.at[x], x_peers[d - 1]) for d in range(1, nx)
    ]
    start(exchange)

    turner = turn(GROUP, BF16)

    def turn_group(k, carry):
        at = pl.multiple_of(k * GROUP, GROUP)
        turned = mm(turner, a_buf[pl.ds(REACH + at, GROUP), :])
        t_buf[pl.ds(at, GROUP), :] = turned.astype(BF16)
        return carry

    lax.fori_loop(0, TASK // GROUP, turn_group, 0, unroll=4)

    to_after, to_before = [], []
    for c in range(4):
        at, size = c * 8 * WF, 8 * WF
        to_after.append(remote(t_buf.at[pl.ds(at, size)], rp_buf.at[pl.ds(at, size)], after))
        at, size = (0, 12 * WF) if c == 0 else ((4 + 8 * c) * WF, 8 * WF)
        to_before.append(remote(a_buf.at[pl.ds(TASK + at, size)], rn_buf.at[pl.ds(at, size)], before))

    def not_first(action):
        pl.when(t > 0)(action)

    def not_last(action):
        pl.when(t < frames - 1)(action)

    bias = b_in_ref[...]
    ready = set()
    strips = []

    def await_part(view, c):
        if (view, c) not in ready:
            ready.add((view, c))
            if view == 0:
                not_first(to_after[c].wait_recv)
            else:
                not_last(to_before[c].wait_recv)

    def meanwhile(point):
        for kind, low, high in SCHEDULE.get(point, ()):
            if kind == "send":
                for c in range(low, high):
                    not_first(to_before[c].start)
                    not_last(to_after[c].start)
            elif kind == "upper":
                for c in range((high + 1) // 2):
                    await_part(0, c)
                hidden_rows(low, high, rp_buf, 0, a_buf, 0, band, bias, hid.at[0])
                if high == TASK // GROUP:
                    strip_send[...] = flow_rows(hid.at[0], conv[...], 0)
                    strips.append(remote(strip_send, strip_recv, before))
                    start(strips)
            else:
                for c in range(min(3, high // 2) + 1):
                    await_part(1, c)
                hidden_rows(low, high, t_buf, TASK, rn_buf, 0, band, bias, hid.at[1])
                if high == TASK // GROUP:
                    strip_own[...] = flow_rows(hid.at[1], conv[...], 128)

    meanwhile("exchange")
    got1[x] = pooled[x]
    arrived(exchange)
    exchange = []
    for d in range(nx):
        for view, targets in ((core, [None] + y_peers), (other, [partner] + y_partners)):
            if targets[d] is not None:
                source = got1.at[:, around(y, d, nx), view]
                exchange.append(remote(source, got.at[core, :, y], targets[d]))
    start(exchange)
    meanwhile("exchange 2")
    got[core, :, y] = got1[:, y, core]
    lax.fori_loop(TASK // GROUP, 2 * (TASK // GROUP), turn_group, 0, unroll=4)
    band[0] = band_weights(w_in_ref[...], 0)
    band[1] = band_weights(w_in_ref[...], 1)
    conv[...] = conv_weights(w_out_ref)
    arrived(exchange)
    meanwhile("embed")

    total = [jnp.zeros((1, 256), F32) for _ in range(EXP // 256)]
    for clip in range(2):
        features = got[clip].reshape(rows, D_FEAT)
        mixed = (mm(mixer[0], features) + mm(mixer[1], features)).astype(BF16)
        for k in range(EXP // 256):
            cols = pl.ds(k * 256, 256)
            value = gelu(mm(mixed, ew_ref[:, cols]) + eb_ref[:, cols]).astype(BF16)
            z_buf[pl.ds(clip * rows, rows), cols] = value
            total[k] = total[k] + jnp.sum(value.astype(F32), axis=0, keepdims=True)
    mean = jnp.concatenate(total, axis=1) / local_rows
    mean0[0] = mean
    share_x = [remote(mean0.at[0], mean_x.at[d - 1], x_peers[d - 1]) for d in range(1, nx)]
    share_y = [remote(mean0.at[0], mean_y.at[d - 1], y_peers[d - 1]) for d in range(1, nx)]
    start(share_x)
    start(share_y)

    def center(k, carry):
        part = pl.ds(pl.multiple_of(k * 64, 64), 64)
        zc_buf[part, :] = (z_buf[part, :].astype(F32) - mean).astype(BF16)
        return carry

    lax.fori_loop(0, local_rows // 64, center, 0)
    for k in range(EXP // 256):
        zt_buf[pl.ds(k * 256, 256), :] = zc_buf[:, pl.ds(k * 256, 256)].T
    left, right = pl.ds(0, HALF), pl.ds(HALF, HALF)

    for k in range(HALF // 256):
        cols = pl.ds(HALF + k * 256, 256)
        cross = mm(zt_buf[left, :], zc_buf[:, cols]).astype(BF16)
        for j in range(256 // lb):
            send_1[0, k * (256 // lb) + j] = cross[:, j * lb : (j + 1) * lb]
    first_x = [
        remote(send_1.at[0, around(x, d, nx)], recv_1.at[0, d - 1], x_peers[d - 1])
        for d in range(1, nx)
    ]
    start(first_x)
    row_at, col_at = iota((HALF, 256), 0), iota((HALF, 256), 1)
    for k in range(HALF // 256):
        in_left = mm(zt_buf[left, :], zc_buf[:, pl.ds(k * 256, 256)])
        in_right = mm(zt_buf[right, :], zc_buf[:, pl.ds(HALF + k * 256, 256)])
        ahead = col_at + k * 256 - row_at
        both = jnp.where(ahead > 0, in_left, jnp.where(ahead < 0, in_right, 0.0)).astype(BF16)
        for j in range(256 // lb):
            send_1[1, k * (256 // lb) + j] = both[:, j * lb : (j + 1) * lb]
    first_y = [
        remote(send_1.at[1, around(y, d, nx)], recv_1.at[1, d - 1], y_peers[d - 1])
        for d in range(1, nx)
    ]
    start(first_y)
    meanwhile("first")

    def combine(own, parts, n):
        center = own
        for i in range(n - 1):
            center = center + parts[i]
        center = center / n
        lines = [own - center] + [parts[i] - center for i in range(n - 1)]
        lines += [jnp.zeros_like(own)] * (8 - n)
        dev[...] = jnp.concatenate(lines, axis=0)
        return center

    def outer(first_at, height, second_at):
        return mm(
            dev[:, pl.ds(first_at, height)],
            dev[:, pl.ds(second_at, lb)],
            TN,
            precision=lax.Precision.HIGHEST,
        )

    def triangles(first_at, height, block_at, inner_at):
        in_left = outer(first_at, height, block_at)
        in_right = outer(HALF + first_at, height, HALF + block_at)
        ahead = (block_at + iota((height, lb), 1)) - (inner_at + iota((height, lb), 0))
        return jnp.where(ahead > 0, in_left, jnp.where(ahead < 0, in_right, 0.0))

    x_at, y_at = pl.multiple_of(x * lb, lb), pl.multiple_of(y * lb, lb)

    arrived(share_x)
    center_x = combine(mean0[0], mean_x, nx)
    mean1[0] = center_x
    carry_x = [remote(mean1.at[0], mean_x2.at[d - 1], y_peers[d - 1]) for d in range(1, nx)]
    start(carry_x)
    part = local_rows * outer(0, HALF, HALF + x_at)
    arrived(first_x)
    part = part + send_1[0, x].astype(F32)
    for i in range(nx - 1):
        part = part + recv_1[0, i].astype(F32)
    send_2[0] = part.astype(BF16)
    second_x = [
        remote(
            send_2.at[0, pl.ds(pl.multiple_of(around(y, d, nx) * lb, lb), lb)],
            recv_2.at[0, d - 1],
            y_peers[d - 1],
        )
        for d in range(1, nx)
    ]
    start(second_x)

    arrived(share_y)
    center_y = combine(mean0[0], mean_y, nx)
    mean1[1] = center_y
    carry_y = [remote(mean1.at[1], mean_y2.at[d - 1], x_peers[d - 1]) for d in range(1, nx)]
    start(carry_y)
    part = local_rows * triangles(0, HALF, y_at, 0)
    arrived(first_y)
    part = part + send_1[1, y].astype(F32)
    for i in range(nx - 1):
        part = part + recv_1[1, i].astype(F32)
    send_2[1] = part.astype(BF16)
    second_y = [
        remote(
            send_2.at[1, pl.ds(pl.multiple_of(around(x, d, nx) * lb, lb), lb)],
            recv_2.at[1, d - 1],
            x_peers[d - 1],
        )
        for d in range(1, nx)
    ]
    start(second_y)
    meanwhile("second")

    arrived(carry_x)
    center_xy = combine(mean1[0], mean_x2, nx)
    mean2[0] = center_xy
    carry_z = [remote(mean2.at[0], mean_z.at[d - 1], z_peers[d - 1]) for d in range(1, nz)]
    start(carry_z)
    part = (local_rows * nx) * outer(y_at, lb, HALF + x_at)
    arrived(second_x)
    part = part + send_2[0, pl.ds(y_at, lb)].astype(F32)
    for i in range(nx - 1):
        part = part + recv_2[0, i].astype(F32)
    send_3[0] = part.astype(BF16)

    arrived(carry_y)
    combine(mean1[1], mean_y2, nx)
    part = (local_rows * nx) * triangles(x_at, lb, y_at, x_at)
    arrived(second_y)
    part = part + send_2[1, pl.ds(x_at, lb)].astype(F32)
    for i in range(nx - 1):
        part = part + recv_2[1, i].astype(F32)
    send_3[1] = part.astype(BF16)

    def z_rows(i):
        return pl.ds(pl.multiple_of(i * zr, zr), zr)

    third = [
        remote(send_3.at[:, z_rows(around(z, d, nz))], recv_3.at[d - 1], z_peers[d - 1])
        for d in range(1, nz)
    ]
    start(third)
    meanwhile("third")
    arrived(carry_z)
    mean = combine(mean2[0], mean_z, nz)
    group_rows = local_rows * frames
    small[0] = group_rows * outer(y_at, lb, HALF + x_at)
    small[1] = group_rows * triangles(x_at, lb, y_at, x_at)
    arrived(third)
    part = small[:, z_rows(z), :] + send_3[:, z_rows(z), :].astype(F32)
    for i in range(nz - 1):
        part = part + recv_3[i].astype(F32)
    scale = 1.0 / (group_rows * nz - 1) / math.sqrt(EXP)
    cov_z[:, z_rows(z), :] = (part * scale).astype(BF16)

    back_z = [
        remote(cov_z.at[:, z_rows(z)], cov_z.at[:, z_rows(z)], z_peers[d - 1])
        for d in range(1, nz)
    ]
    start(back_z)

    def center_all(k, carry):
        part = pl.ds(pl.multiple_of(k * 64, 64), 64)
        zc_buf[part, :] = (z_buf[part, :].astype(F32) - mean).astype(BF16)
        return carry

    lax.fori_loop(0, local_rows // 64, center_all, 0)
    meanwhile("back z")
    arrived(back_z)
    y_rows, x_rows = pl.ds(y_at, lb), pl.ds(x_at, lb)
    back_2 = [
        remote(cov_z.at[0], cov_mid.at[0, y_rows], y_peers[d - 1]) for d in range(1, nx)
    ] + [remote(cov_z.at[1], cov_mid.at[1, x_rows], x_peers[d - 1]) for d in range(1, nx)]
    start(back_2)
    cov_mid[0, y_rows] = cov_z[0]
    cov_mid[1, x_rows] = cov_z[1]
    meanwhile("back 2")
    arrived(back_2)
    back_1 = [
        remote(cov_mid.at[0], cov_all.at[0, x], x_peers[d - 1]) for d in range(1, nx)
    ] + [remote(cov_mid.at[1], cov_all.at[1, y], y_peers[d - 1]) for d in range(1, nx)]
    start(back_1)
    cov_all[0, x] = cov_mid[0]
    cov_all[1, y] = cov_mid[1]

    meanwhile("back 1")

    arrived(back_1)
    pieces = HALF // lb
    cross = jnp.concatenate([cov_all[0, k] for k in range(pieces)], axis=1)
    both = jnp.concatenate([cov_all[1, k] for k in range(pieces)], axis=1)
    turned = both.T
    ahead = iota((HALF, HALF), 1) - iota((HALF, HALF), 0)
    matrix[left, right] = cross
    matrix[right, left] = cross.T
    matrix[left, left] = jnp.where(ahead > 0, both, turned)
    matrix[right, right] = jnp.where(ahead < 0, both, turned)

    def gradient(slot, clip):
        lines = pl.ds(pl.multiple_of(clip * rows, rows), rows)
        for k in range(2):
            for j in range(2):
                cols = pl.ds(k * HALF + j * 256, 256)
                grads[slot, :, cols] = mm(zc_buf[lines, :], matrix[:, cols]).astype(BF16)
            cols = pl.ds(k * HALF, HALF)
            if slot == 0:
                copy = remote(grads.at[0, :, cols], grad_ref.at[core, :, cols], partner)
                start([copy])
            else:
                copy = pltpu.make_async_copy(
                    grads.at[1, :, cols], grad_ref.at[core, :, cols], local_sem.at[2 + k]
                )
                copy.start()
            results.append(copy)

    results = []
    gradient(0, other)
    gradient(1, core)

    arrived(strips)
    edge = STRIP - 256
    top, bottom = strip_recv[...], strip_own[...]
    flow_ref[:, 0:edge] = top[0:2, :edge]
    flow_ref[:, edge:STRIP] = top[0:2, edge:] + bottom[0:2, :256]
    flow_ref[:, STRIP:] = bottom[0:2, 256:]

    for copy in results:
        copy.wait_recv()
    for c in range(4):
        not_first(to_before[c].wait_send)
        not_last(to_after[c].wait_send)
    for copy in started:
        copy.wait_send()


def hand_out(flow_in, grads_in, flow_out, grads_out, held, in_sem, out_sem):
    loads, stores = [], []
    for k in range(4):
        part = (k // 2, pl.ds((k % 2) * 128, 128))
        loads.append(pltpu.make_async_copy(grads_in.at[part], held.at[part], in_sem.at[k]))
        stores.append(pltpu.make_async_copy(held.at[part], grads_out.at[part], out_sem.at[k]))
        loads[k].start()
    flow_out[...] = flow_in[...]
    for k in range(4):
        loads[k].wait()
        stores[k].start()
    for k in range(4):
        stores[k].wait()


def on_device(
    nx,
    nz,
    feat_a,
    feat_b,
    flow_in_weight,
    flow_entry_bias,
    flow_out_weight,
    frame_mix,
    expand_weight,
    expand_bias,
):
    frames = nx * nx
    block = POOLED // frames
    rows = frames * block
    lb = HALF // nx
    zr = lb // nz
    copies = 3 * nx + 8 + 18 * (nx - 1) + 3 * (nz - 1) + 3
    vmem = pl.BlockSpec(memory_space=pltpu.VMEM)
    hbm = pl.BlockSpec(memory_space=pl.ANY)
    scratch = [
        pltpu.VMEM((REACH + POSITIONS, D_FEAT), BF16),
        pltpu.VMEM((POSITIONS, D_FEAT), BF16),
        pltpu.VMEM((POSITIONS, D_FEAT), BF16),
        pltpu.VMEM((NEXT_ROWS, D_FEAT), BF16),
        pltpu.VMEM((TASK, D_FEAT), BF16),
        pltpu.VMEM((2, 640, DEC), BF16),
        pltpu.VMEM((32, DEC), BF16),
        pltpu.VMEM((2, rows, rows), BF16),
        pltpu.VMEM((nx, nx, 2, block, D_FEAT), BF16),
        pltpu.VMEM((nx, nx, 2, block, D_FEAT), BF16),
        pltpu.VMEM((2, nx, nx, block, D_FEAT), BF16),
        pltpu.VMEM((2 * rows, EXP), BF16),
        pltpu.VMEM((2 * rows, EXP), BF16),
        pltpu.VMEM((EXP, 2 * rows), BF16),
        pltpu.VMEM((1, 1, EXP), F32),
        pltpu.VMEM((nx - 1, 1, EXP), F32),
        pltpu.VMEM((nx - 1, 1, EXP), F32),
        pltpu.VMEM((2, 1, EXP), F32),
        pltpu.VMEM((nx - 1, 1, EXP), F32),
        pltpu.VMEM((nx - 1, 1, EXP), F32),
        pltpu.VMEM((1, 1, EXP), F32),
        pltpu.VMEM((nz - 1, 1, EXP), F32),
        pltpu.VMEM((8, EXP), F32),
        pltpu.VMEM((2, nx, HALF, lb), BF16),
        pltpu.VMEM((2, nx - 1, HALF, lb), BF16),
        pltpu.VMEM((2, HALF, lb), BF16),
        pltpu.VMEM((2, nx - 1, lb, lb), BF16),
        pltpu.VMEM((2, lb, lb), BF16),
        pltpu.VMEM((nz - 1, 2, zr, lb), BF16),
        pltpu.VMEM((2, lb, lb), F32),
        pltpu.VMEM((2, lb, lb), BF16),
        pltpu.VMEM((2, HALF, lb), BF16),
        pltpu.VMEM((2, nx, HALF, lb), BF16),
        pltpu.VMEM((EXP, EXP), BF16),
        pltpu.VMEM((2, TASK, DEC), BF16),
        pltpu.VMEM((8, STRIP), F32),
        pltpu.VMEM((8, STRIP), F32),
        pltpu.VMEM((8, STRIP), F32),
        pltpu.VMEM((2, rows, EXP), BF16),
        pltpu.SemaphoreType.DMA((4,)),
        pltpu.SemaphoreType.DMA((copies,)),
        pltpu.SemaphoreType.DMA((copies,)),
    ]
    flow, grads = pl.pallas_call(
        functools.partial(kernel, nx, nz),
        out_shape=[
            jax.ShapeDtypeStruct((2, POSITIONS), F32),
            jax.ShapeDtypeStruct((2, rows, EXP), BF16),
        ],
        in_specs=[hbm, hbm] + [vmem] * 6,
        out_specs=[vmem, hbm],
        scratch_shapes=scratch,
        compiler_params=pltpu.CompilerParams(
            collective_id=0, has_side_effects=True, vmem_limit_bytes=56 * 1024 * 1024
        ),
    )(
        feat_a,
        feat_b,
        flow_in_weight.T,
        flow_entry_bias.reshape(1, DEC),
        flow_out_weight,
        frame_mix,
        expand_weight,
        expand_bias.reshape(1, EXP),
    )
    flow, grads = pl.pallas_call(
        hand_out,
        out_shape=[
            jax.ShapeDtypeStruct((2, POSITIONS), F32),
            jax.ShapeDtypeStruct((2, rows, EXP), BF16),
        ],
        in_specs=[vmem, hbm],
        out_specs=[vmem, hbm],
        scratch_shapes=[
            pltpu.VMEM((2, rows, EXP), BF16),
            pltpu.SemaphoreType.DMA((4,)),
            pltpu.SemaphoreType.DMA((4,)),
        ],
    )(flow, grads)
    return (
        flow.reshape(1, 1, 2, POSITIONS),
        grads.reshape(2, 1, frames, block, EXP),
    )


def solution(mesh):
    nx = math.isqrt(mesh.shape["tm"])
    nz = mesh.shape["batch"] // 2
    return jax.shard_map(
        functools.partial(on_device, nx, nz),
        mesh=mesh,
        in_specs=(
            P("batch", "tm", None, None),
            P("batch", "tm", None, None),
            P(),
            P(),
            P(),
            P(),
            P(),
            P(),
        ),
        out_specs=(P("batch", "tm", None, None), P(None, "batch", None, "tm", None)),
        check_vma=False,
    )
```

```python
import functools
import math

import jax
import jax.numpy as jnp
from jax import lax
from jax.experimental import pallas as pl
from jax.experimental.pallas import tpu as pltpu
from jax.sharding import PartitionSpec as P

MESH = pl.DeviceIdType.MESH
F32 = jnp.float32
BF16 = jnp.bfloat16

HF = 64
WF = 64
D_FEAT = 256
EXP = 1024
HALF = EXP // 2
DEC = 128
DISP = 81
POSITIONS = HF * WF
POOLED = 256
GROUP = 4 * WF
TASK = 32 * WF
REACH = 4 * WF
NEXT_ROWS = TASK + 2 * REACH
UNROLL = 2
STRIP = 34 * WF

SCHEDULE = {
    "embed": [("send", 0, 1)],
    "first": [("send", 1, 2)],
    "second": [("send", 2, 3)],
    "third": [("send", 3, 4), ("upper", 0, 2), ("lower", 0, 1)],
    "back z": [("upper", 2, 4), ("lower", 1, 3)],
    "back 2": [("upper", 4, 6), ("lower", 3, 5)],
    "back 1": [("upper", 6, 8), ("lower", 5, 8)],
}

NN = (((1,), (0,)), ((), ()))
NT = (((1,), (1,)), ((), ()))
TN = (((0,), (0,)), ((), ()))


def mm(a, b, dims=NN, precision=None):
    return lax.dot_general(a, b, dims, precision=precision, preferred_element_type=F32)


def iota(shape, axis):
    return lax.broadcasted_iota(jnp.int32, shape, axis)


def gelu(x):
    return 0.5 * x * (1.0 + jnp.tanh(math.sqrt(2.0 / math.pi) * (x + 0.044715 * (x * x * x))))


def one_hot(condition):
    return jnp.where(condition, 1.0, 0.0).astype(BF16)


def turn(size, kind):
    hit = (iota((size, size), 0) ^ 63) == iota((size, size), 1)
    return jnp.where(hit, 1.0, 0.0).astype(kind)


def band_weights(w_in, odd):
    shape = (5 * 128, DISP)
    row, col = iota(shape, 0), iota(shape, 1)
    lane = (row + 4) & 127
    dy = (row >> 7) * 2 + 1 - (lane >> 6) - odd
    dx = lane & 63
    hit = (dx < 9) & (dy >= 0) & (dy < 9) & (dy * 9 + dx == col)
    return (mm(one_hot(hit), w_in.astype(BF16)) * (1.0 / math.sqrt(D_FEAT))).astype(BF16)


def conv_weights(w_out_ref):
    zeros = jnp.zeros((2, DEC), F32)
    rows = []
    for kx in (2, 1, 0):
        rows += [w_out_ref[ky, kx] for ky in range(3)] + [zeros]
    rows += [jnp.zeros((8, DEC), F32)]
    return jnp.concatenate(rows, axis=0).astype(BF16)


def mixing_weights(mix, frames, block):
    size = frames * block
    spread = one_hot(lax.div(iota((size, frames), 0), block) == iota((size, frames), 1))
    same = lax.rem(iota((size, size), 0), block) == lax.rem(iota((size, size), 1), block)
    high = mix.astype(BF16)
    low = (mix - high.astype(F32)).astype(BF16)
    parts = []
    for part in (high, low):
        rows = mm(spread, part).astype(BF16)
        parts.append(jnp.where(same, mm(rows, spread, NT), 0.0).astype(BF16))
    return parts


def hidden_rows(low, high, first_ref, first_at, next_ref, next_at, band_ref, bias, hid_ref):
    x, lane = 63 - iota((WF, 128), 0), (iota((WF, 128), 1) + 4) & 63
    inside = (lane < 9) & (x + lane >= 4) & (x + lane < WF + 4)

    def group(g, carry):
        at = pl.multiple_of(g * GROUP, GROUP)
        first = first_ref[pl.ds(first_at + at, GROUP), :]
        latter = next_ref[pl.ds(next_at + at, 3 * GROUP), :]
        products = mm(first, latter, NT)
        for odd in range(2):
            pieces = []
            for i in (odd, odd + 2):
                blocks = []
                for m in range(i // 2, i // 2 + 5):
                    block = products[i * WF : (i + 1) * WF, m * 128 : (m + 1) * 128]
                    block = pltpu.roll(block, 1, 1, stride=1, stride_axis=0)
                    blocks.append(jnp.where(inside, block, 0.0).astype(BF16))
                pieces.append(jnp.concatenate(blocks, axis=1))
            skewed = jnp.concatenate(pieces, axis=0)
            hidden = gelu(mm(skewed, band_ref[odd]) + bias).astype(BF16)
            hid_ref[pl.ds(at + odd * WF, WF), :] = hidden[:WF]
            hid_ref[pl.ds(at + (odd + 2) * WF, WF), :] = hidden[WF:]
        return carry

    lax.fori_loop(low, high, group, 0, unroll=UNROLL)


def flow_rows(hid_ref, conv, base):
    taps = mm(conv, hid_ref[...], NT)
    lane = iota((8, TASK), 1) & 63
    across = (
        taps[8:16]
        + jnp.where(lane != 0, pltpu.roll(taps[0:8], 1, 1), 0.0)
        + jnp.where(lane != 63, pltpu.roll(taps[16:24], TASK - 1, 1), 0.0)
    )
    wide = TASK + 256
    across = jnp.concatenate([across, jnp.zeros((8, 256), F32)], axis=1)
    total = pltpu.roll(across, base + 64, 1)
    middle = pltpu.roll(across, base, 1) if base else across
    total = total + pltpu.roll(middle, 6, 0)
    total = total + pltpu.roll(pltpu.roll(across, (base + wide - 64) % wide, 1), 4, 0)
    blocks = [total[:, k * 128 : (k + 1) * 128] for k in range(STRIP // 128)]
    turned = mm(jnp.concatenate(blocks, axis=0), turn(128, F32), precision=lax.Precision.HIGHEST)
    return jnp.concatenate([turned[k * 8 : (k + 1) * 8] for k in range(STRIP // 128)], axis=1)


def kernel(
    nx,
    nz,
    fa_ref,
    fb_ref,
    w_in_any,
    b_in_any,
    w_out_any,
    mix_any,
    ew_any,
    eb_any,
    flow_any,
    grad_ref,
    w_in_ref,
    b_in_ref,
    w_out_ref,
    mix_ref,
    ew_ref,
    eb_ref,
    flow_ref,
    a_buf,
    b_buf,
    t_buf,
    rn_buf,
    rp_buf,
    band,
    conv,
    mixer,
    pooled,
    got,
    z_buf,
    zc_buf,
    zt_buf,
    mean0,
    mean_x,
    mean_y,
    mean1,
    mean_x2,
    mean_y2,
    mean2,
    mean_z,
    dev,
    send_1,
    recv_1,
    send_2,
    recv_2,
    send_3,
    recv_3,
    small,
    cov_z,
    cov_mid,
    cov_all,
    matrix,
    hid,
    strip_send,
    strip_recv,
    strip_own,
    grads,
    local_sem,
    send_sem,
    recv_sem,
):
    frames = nx * nx
    block = POOLED // frames
    rows = frames * block
    local_rows = 2 * rows
    lb = HALF // nx
    zr = lb // nz

    batch, t = lax.axis_index("batch"), lax.axis_index("tm")
    z, core = lax.div(batch, 2), lax.rem(batch, 2)
    x, y = lax.div(t, nx), lax.rem(t, nx)
    other = 1 - core

    def around(i, d, n):
        return lax.rem(i + d, n)

    x_peers = [(batch, around(x, d, nx) * nx + y) for d in range(1, nx)]
    y_peers = [(batch, x * nx + around(y, d, nx)) for d in range(1, nx)]
    z_peers = [(around(z, d, nz) * 2 + core, t) for d in range(1, nz)]
    partner = (z * 2 + other, t)
    before = (batch, lax.rem(t + frames - 1, frames))
    after = (batch, lax.rem(t + 1, frames))

    count = [0]

    def remote(src, dst, device):
        i = count[0]
        count[0] += 1
        return pltpu.make_async_remote_copy(
            src_ref=src,
            dst_ref=dst,
            send_sem=send_sem.at[i],
            recv_sem=recv_sem.at[i],
            device_id=device,
            device_id_type=MESH,
        )

    def start(copies):
        for copy in copies:
            copy.start()
        started.extend(copies)

    def arrived(copies):
        for copy in copies:
            copy.wait_recv()

    started = []

    barrier = pltpu.get_barrier_semaphore()
    for device in z_peers + [partner]:
        pl.semaphore_signal(barrier, inc=1, device_id=device, device_id_type=MESH)

    def greet(d, carry):
        for c in range(2):
            device = (z * 2 + c, around(t, d, frames))
            pl.semaphore_signal(barrier, inc=1, device_id=device, device_id_type=MESH)
        return carry

    lax.fori_loop(1, frames, greet, 0)
    load_a = pltpu.make_async_copy(fa_ref.at[0, 0], a_buf.at[pl.ds(REACH, POSITIONS)], local_sem.at[0])
    load_b = pltpu.make_async_copy(fb_ref.at[0, 0], b_buf, local_sem.at[1])
    load_mix = pltpu.make_async_copy(mix_any, mix_ref, local_sem.at[4])
    load_mix.start()
    load_a.start()
    load_b.start()
    loads = []
    for i, (source, target) in enumerate(
        [(w_in_any, w_in_ref), (b_in_any, b_in_ref), (w_out_any, w_out_ref), (ew_any, ew_ref), (eb_any, eb_ref)]
    ):
        loads.append(pltpu.make_async_copy(source, target, local_sem.at[5 + i]))
        loads[i].start()

    a_buf[pl.ds(0, REACH), :] = jnp.zeros((REACH, D_FEAT), BF16)
    rn_buf[pl.ds(TASK + REACH, REACH), :] = jnp.zeros((REACH, D_FEAT), BF16)

    @pl.when(t == frames - 1)
    def _():
        rn_buf[pl.ds(0, TASK + REACH), :] = jnp.zeros((TASK + REACH, D_FEAT), BF16)

    @pl.when(t == 0)
    def _():
        rp_buf[...] = jnp.zeros((TASK, D_FEAT), BF16)

    load_mix.wait()
    mixer[0], mixer[1] = mixing_weights(mix_ref[...], frames, block)

    span = POSITIONS // frames
    prow, pcol = iota((block, span), 0), iota((block, span), 1)
    pooled_at = lax.div(pcol, GROUP) * 16 + lax.div(pcol & 63, 4)
    pool = one_hot(pooled_at == prow)
    load_a.wait()
    load_b.wait()

    def pool_block(k, carry):
        at = pl.multiple_of(k * span, span)
        from_a = mm(pool, a_buf[pl.ds(REACH + at, span), :]) * (1.0 / 16.0)
        pooled[k, 0] = from_a.astype(BF16)
        from_b = mm(pool, b_buf[pl.ds(at, span), :]) * (1.0 / 16.0)
        pooled[k, 1] = from_b.astype(BF16)
        return carry

    lax.fori_loop(0, frames, pool_block, 0)
    for load in loads:
        load.wait()
    pl.semaphore_wait(barrier, nz - 1 + 1 + 2 * (frames - 1))

    exchange = []
    for d in range(frames):
        to = around(t, d, frames)
        for view, device in ((core, (batch, to)), (other, (z * 2 + other, to))):
            if d > 0 or view is other:
                exchange.append(remote(pooled.at[to, view], got.at[core, t], device))
    start(exchange)

    turner = turn(GROUP, BF16)

    def turn_group(k, carry):
        at = pl.multiple_of(k * GROUP, GROUP)
        turned = mm(turner, a_buf[pl.ds(REACH + at, GROUP), :])
        t_buf[pl.ds(at, GROUP), :] = turned.astype(BF16)
        return carry

    lax.fori_loop(0, TASK // GROUP, turn_group, 0, unroll=4)

    to_after, to_before = [], []
    for c in range(4):
        at, size = c * 8 * WF, 8 * WF
        to_after.append(remote(t_buf.at[pl.ds(at, size)], rp_buf.at[pl.ds(at, size)], after))
        at, size = (0, 12 * WF) if c == 0 else ((4 + 8 * c) * WF, 8 * WF)
        to_before.append(remote(a_buf.at[pl.ds(TASK + at, size)], rn_buf.at[pl.ds(at, size)], before))

    def not_first(action):
        pl.when(t > 0)(action)

    def not_last(action):
        pl.when(t < frames - 1)(action)

    bias = b_in_ref[...]
    ready = set()
    strips = []

    def await_part(view, c):
        if (view, c) not in ready:
            ready.add((view, c))
            if view == 0:
                not_first(to_after[c].wait_recv)
            else:
                not_last(to_before[c].wait_recv)

    def meanwhile(point):
        for kind, low, high in SCHEDULE.get(point, ()):
            if kind == "send":
                for c in range(low, high):
                    not_first(to_before[c].start)
                    not_last(to_after[c].start)
            elif kind == "upper":
                for c in range((high + 1) // 2):
                    await_part(0, c)
                hidden_rows(low, high, rp_buf, 0, a_buf, 0, band, bias, hid.at[0])
                if high == TASK // GROUP:
                    strip_send[...] = flow_rows(hid.at[0], conv[...], 0)
                    strips.append(remote(strip_send, strip_recv, before))
                    start(strips)
            else:
                for c in range(min(3, high // 2) + 1):
                    await_part(1, c)
                hidden_rows(low, high, t_buf, TASK, rn_buf, 0, band, bias, hid.at[1])
                if high == TASK // GROUP:
                    strip_own[...] = flow_rows(hid.at[1], conv[...], 128)

    meanwhile("exchange")
    got[core, t] = pooled[t, core]
    lax.fori_loop(TASK // GROUP, 2 * (TASK // GROUP), turn_group, 0, unroll=4)
    band[0] = band_weights(w_in_ref[...], 0)
    band[1] = band_weights(w_in_ref[...], 1)
    conv[...] = conv_weights(w_out_ref)
    arrived(exchange)
    meanwhile("embed")

    total = [jnp.zeros((1, 256), F32) for _ in range(EXP // 256)]
    for clip in range(2):
        features = got[clip].reshape(rows, D_FEAT)
        mixed = (mm(mixer[0], features) + mm(mixer[1], features)).astype(BF16)
        for k in range(EXP // 256):
            cols = pl.ds(k * 256, 256)
            value = gelu(mm(mixed, ew_ref[:, cols]) + eb_ref[:, cols]).astype(BF16)
            z_buf[pl.ds(clip * rows, rows), cols] = value
            total[k] = total[k] + jnp.sum(value.astype(F32), axis=0, keepdims=True)
    mean = jnp.concatenate(total, axis=1) / local_rows
    mean0[0] = mean
    share_x = [remote(mean0.at[0], mean_x.at[d - 1], x_peers[d - 1]) for d in range(1, nx)]
    share_y = [remote(mean0.at[0], mean_y.at[d - 1], y_peers[d - 1]) for d in range(1, nx)]
    start(share_x)
    start(share_y)

    def center(k, carry):
        part = pl.ds(pl.multiple_of(k * 64, 64), 64)
        zc_buf[part, :] = (z_buf[part, :].astype(F32) - mean).astype(BF16)
        return carry

    lax.fori_loop(0, local_rows // 64, center, 0)
    for k in range(EXP // 256):
        zt_buf[pl.ds(k * 256, 256), :] = zc_buf[:, pl.ds(k * 256, 256)].T
    left, right = pl.ds(0, HALF), pl.ds(HALF, HALF)

    for k in range(HALF // 256):
        cols = pl.ds(HALF + k * 256, 256)
        cross = mm(zt_buf[left, :], zc_buf[:, cols]).astype(BF16)
        for j in range(256 // lb):
            send_1[0, k * (256 // lb) + j] = cross[:, j * lb : (j + 1) * lb]
    first_x = [
        remote(send_1.at[0, around(x, d, nx)], recv_1.at[0, d - 1], x_peers[d - 1])
        for d in range(1, nx)
    ]
    start(first_x)
    row_at, col_at = iota((HALF, 256), 0), iota((HALF, 256), 1)
    for k in range(HALF // 256):
        in_left = mm(zt_buf[left, :], zc_buf[:, pl.ds(k * 256, 256)])
        in_right = mm(zt_buf[right, :], zc_buf[:, pl.ds(HALF + k * 256, 256)])
        ahead = col_at + k * 256 - row_at
        both = jnp.where(ahead > 0, in_left, jnp.where(ahead < 0, in_right, 0.0)).astype(BF16)
        for j in range(256 // lb):
            send_1[1, k * (256 // lb) + j] = both[:, j * lb : (j + 1) * lb]
    first_y = [
        remote(send_1.at[1, around(y, d, nx)], recv_1.at[1, d - 1], y_peers[d - 1])
        for d in range(1, nx)
    ]
    start(first_y)
    meanwhile("first")

    def combine(own, parts, n):
        center = own
        for i in range(n - 1):
            center = center + parts[i]
        center = center / n
        lines = [own - center] + [parts[i] - center for i in range(n - 1)]
        lines += [jnp.zeros_like(own)] * (8 - n)
        dev[...] = jnp.concatenate(lines, axis=0)
        return center

    def outer(first_at, height, second_at):
        return mm(
            dev[:, pl.ds(first_at, height)],
            dev[:, pl.ds(second_at, lb)],
            TN,
            precision=lax.Precision.HIGHEST,
        )

    def triangles(first_at, height, block_at, inner_at):
        in_left = outer(first_at, height, block_at)
        in_right = outer(HALF + first_at, height, HALF + block_at)
        ahead = (block_at + iota((height, lb), 1)) - (inner_at + iota((height, lb), 0))
        return jnp.where(ahead > 0, in_left, jnp.where(ahead < 0, in_right, 0.0))

    x_at, y_at = pl.multiple_of(x * lb, lb), pl.multiple_of(y * lb, lb)

    arrived(share_x)
    center_x = combine(mean0[0], mean_x, nx)
    mean1[0] = center_x
    carry_x = [remote(mean1.at[0], mean_x2.at[d - 1], y_peers[d - 1]) for d in range(1, nx)]
    start(carry_x)
    part = local_rows * outer(0, HALF, HALF + x_at)
    arrived(first_x)
    part = part + send_1[0, x].astype(F32)
    for i in range(nx - 1):
        part = part + recv_1[0, i].astype(F32)
    send_2[0] = part.astype(BF16)
    second_x = [
        remote(
            send_2.at[0, pl.ds(pl.multiple_of(around(y, d, nx) * lb, lb), lb)],
            recv_2.at[0, d - 1],
            y_peers[d - 1],
        )
        for d in range(1, nx)
    ]
    start(second_x)

    arrived(share_y)
    center_y = combine(mean0[0], mean_y, nx)
    mean1[1] = center_y
    carry_y = [remote(mean1.at[1], mean_y2.at[d - 1], x_peers[d - 1]) for d in range(1, nx)]
    start(carry_y)
    part = local_rows * triangles(0, HALF, y_at, 0)
    arrived(first_y)
    part = part + send_1[1, y].astype(F32)
    for i in range(nx - 1):
        part = part + recv_1[1, i].astype(F32)
    send_2[1] = part.astype(BF16)
    second_y = [
        remote(
            send_2.at[1, pl.ds(pl.multiple_of(around(x, d, nx) * lb, lb), lb)],
            recv_2.at[1, d - 1],
            x_peers[d - 1],
        )
        for d in range(1, nx)
    ]
    start(second_y)
    meanwhile("second")

    arrived(carry_x)
    center_xy = combine(mean1[0], mean_x2, nx)
    mean2[0] = center_xy
    carry_z = [remote(mean2.at[0], mean_z.at[d - 1], z_peers[d - 1]) for d in range(1, nz)]
    start(carry_z)
    part = (local_rows * nx) * outer(y_at, lb, HALF + x_at)
    arrived(second_x)
    part = part + send_2[0, pl.ds(y_at, lb)].astype(F32)
    for i in range(nx - 1):
        part = part + recv_2[0, i].astype(F32)
    send_3[0] = part.astype(BF16)

    arrived(carry_y)
    combine(mean1[1], mean_y2, nx)
    part = (local_rows * nx) * triangles(x_at, lb, y_at, x_at)
    arrived(second_y)
    part = part + send_2[1, pl.ds(x_at, lb)].astype(F32)
    for i in range(nx - 1):
        part = part + recv_2[1, i].astype(F32)
    send_3[1] = part.astype(BF16)

    def z_rows(i):
        return pl.ds(pl.multiple_of(i * zr, zr), zr)

    third = [
        remote(send_3.at[:, z_rows(around(z, d, nz))], recv_3.at[d - 1], z_peers[d - 1])
        for d in range(1, nz)
    ]
    start(third)
    meanwhile("third")
    arrived(carry_z)
    mean = combine(mean2[0], mean_z, nz)
    group_rows = local_rows * frames
    small[0] = group_rows * outer(y_at, lb, HALF + x_at)
    small[1] = group_rows * triangles(x_at, lb, y_at, x_at)
    arrived(third)
    part = small[:, z_rows(z), :] + send_3[:, z_rows(z), :].astype(F32)
    for i in range(nz - 1):
        part = part + recv_3[i].astype(F32)
    scale = 1.0 / (group_rows * nz - 1) / math.sqrt(EXP)
    cov_z[:, z_rows(z), :] = (part * scale).astype(BF16)

    back_z = [
        remote(cov_z.at[:, z_rows(z)], cov_z.at[:, z_rows(z)], z_peers[d - 1])
        for d in range(1, nz)
    ]
    start(back_z)

    def center_all(k, carry):
        part = pl.ds(pl.multiple_of(k * 64, 64), 64)
        zc_buf[part, :] = (z_buf[part, :].astype(F32) - mean).astype(BF16)
        return carry

    lax.fori_loop(0, local_rows // 64, center_all, 0)
    meanwhile("back z")
    arrived(back_z)
    y_rows, x_rows = pl.ds(y_at, lb), pl.ds(x_at, lb)
    back_2 = [
        remote(cov_z.at[0], cov_mid.at[0, y_rows], y_peers[d - 1]) for d in range(1, nx)
    ] + [remote(cov_z.at[1], cov_mid.at[1, x_rows], x_peers[d - 1]) for d in range(1, nx)]
    start(back_2)
    cov_mid[0, y_rows] = cov_z[0]
    cov_mid[1, x_rows] = cov_z[1]
    meanwhile("back 2")
    arrived(back_2)
    back_1 = [
        remote(cov_mid.at[0], cov_all.at[0, x], x_peers[d - 1]) for d in range(1, nx)
    ] + [remote(cov_mid.at[1], cov_all.at[1, y], y_peers[d - 1]) for d in range(1, nx)]
    start(back_1)
    cov_all[0, x] = cov_mid[0]
    cov_all[1, y] = cov_mid[1]

    meanwhile("back 1")

    arrived(back_1)
    pieces = HALF // lb
    cross = jnp.concatenate([cov_all[0, k] for k in range(pieces)], axis=1)
    both = jnp.concatenate([cov_all[1, k] for k in range(pieces)], axis=1)
    turned = both.T
    ahead = iota((HALF, HALF), 1) - iota((HALF, HALF), 0)
    matrix[left, right] = cross
    matrix[right, left] = cross.T
    matrix[left, left] = jnp.where(ahead > 0, both, turned)
    matrix[right, right] = jnp.where(ahead < 0, both, turned)

    def gradient(slot, clip):
        lines = pl.ds(pl.multiple_of(clip * rows, rows), rows)
        for k in range(2):
            for j in range(2):
                cols = pl.ds(k * HALF + j * 256, 256)
                grads[slot, :, cols] = mm(zc_buf[lines, :], matrix[:, cols]).astype(BF16)
            cols = pl.ds(k * HALF, HALF)
            if slot == 0:
                copy = remote(grads.at[0, :, cols], grad_ref.at[core, :, cols], partner)
                start([copy])
            else:
                copy = pltpu.make_async_copy(
                    grads.at[1, :, cols], grad_ref.at[core, :, cols], local_sem.at[2 + k]
                )
                copy.start()
            results.append(copy)

    results = []
    gradient(0, other)
    gradient(1, core)

    arrived(strips)
    edge = STRIP - 256
    top, bottom = strip_recv[...], strip_own[...]
    flow_ref[:, 0:edge] = top[0:2, :edge]
    flow_ref[:, edge:STRIP] = top[0:2, edge:] + bottom[0:2, :256]
    flow_ref[:, STRIP:] = bottom[0:2, 256:]
    store = pltpu.make_async_copy(flow_ref, flow_any, local_sem.at[10])
    store.start()

    for copy in results:
        copy.wait_recv()
    store.wait()
    for c in range(4):
        not_first(to_before[c].wait_send)
        not_last(to_after[c].wait_send)
    for copy in started:
        copy.wait_send()


def hand_out(flow_in, grads_in, flow_out, grads_out, flow_held, held, in_sem, out_sem):
    loads, stores = [], []
    for k in range(4):
        part = (k // 2, pl.ds((k % 2) * 128, 128))
        loads.append(pltpu.make_async_copy(grads_in.at[part], held.at[part], in_sem.at[k]))
        stores.append(pltpu.make_async_copy(held.at[part], grads_out.at[part], out_sem.at[k]))
    loads.append(pltpu.make_async_copy(flow_in, flow_held, in_sem.at[4]))
    stores.append(pltpu.make_async_copy(flow_held, flow_out, out_sem.at[4]))
    for load in loads:
        load.start()
    for load, store in zip(loads, stores):
        load.wait()
        store.start()
    for store in stores:
        store.wait()


def on_device(
    nx,
    nz,
    feat_a,
    feat_b,
    flow_in_weight,
    flow_entry_bias,
    flow_out_weight,
    frame_mix,
    expand_weight,
    expand_bias,
):
    frames = nx * nx
    block = POOLED // frames
    rows = frames * block
    lb = HALF // nx
    zr = lb // nz
    copies = 2 * frames - 1 + 8 + 12 * (nx - 1) + 3 * (nz - 1) + 3
    hbm = pl.BlockSpec(memory_space=pl.ANY)
    scratch = [
        pltpu.VMEM((DISP, DEC), F32),
        pltpu.VMEM((1, DEC), F32),
        pltpu.VMEM((3, 3, 2, DEC), F32),
        pltpu.VMEM((frames, frames), F32),
        pltpu.VMEM((D_FEAT, EXP), BF16),
        pltpu.VMEM((1, EXP), F32),
        pltpu.VMEM((2, POSITIONS), F32),
        pltpu.VMEM((REACH + POSITIONS, D_FEAT), BF16),
        pltpu.VMEM((POSITIONS, D_FEAT), BF16),
        pltpu.VMEM((POSITIONS, D_FEAT), BF16),
        pltpu.VMEM((NEXT_ROWS, D_FEAT), BF16),
        pltpu.VMEM((TASK, D_FEAT), BF16),
        pltpu.VMEM((2, 640, DEC), BF16),
        pltpu.VMEM((32, DEC), BF16),
        pltpu.VMEM((2, rows, rows), BF16),
        pltpu.VMEM((frames, 2, block, D_FEAT), BF16),
        pltpu.VMEM((2, frames, block, D_FEAT), BF16),
        pltpu.VMEM((2 * rows, EXP), BF16),
        pltpu.VMEM((2 * rows, EXP), BF16),
        pltpu.VMEM((EXP, 2 * rows), BF16),
        pltpu.VMEM((1, 1, EXP), F32),
        pltpu.VMEM((nx - 1, 1, EXP), F32),
        pltpu.VMEM((nx - 1, 1, EXP), F32),
        pltpu.VMEM((2, 1, EXP), F32),
        pltpu.VMEM((nx - 1, 1, EXP), F32),
        pltpu.VMEM((nx - 1, 1, EXP), F32),
        pltpu.VMEM((1, 1, EXP), F32),
        pltpu.VMEM((nz - 1, 1, EXP), F32),
        pltpu.VMEM((8, EXP), F32),
        pltpu.VMEM((2, nx, HALF, lb), BF16),
        pltpu.VMEM((2, nx - 1, HALF, lb), BF16),
        pltpu.VMEM((2, HALF, lb), BF16),
        pltpu.VMEM((2, nx - 1, lb, lb), BF16),
        pltpu.VMEM((2, lb, lb), BF16),
        pltpu.VMEM((nz - 1, 2, zr, lb), BF16),
        pltpu.VMEM((2, lb, lb), F32),
        pltpu.VMEM((2, lb, lb), BF16),
        pltpu.VMEM((2, HALF, lb), BF16),
        pltpu.VMEM((2, nx, HALF, lb), BF16),
        pltpu.VMEM((EXP, EXP), BF16),
        pltpu.VMEM((2, TASK, DEC), BF16),
        pltpu.VMEM((8, STRIP), F32),
        pltpu.VMEM((8, STRIP), F32),
        pltpu.VMEM((8, STRIP), F32),
        pltpu.VMEM((2, rows, EXP), BF16),
        pltpu.SemaphoreType.DMA((11,)),
        pltpu.SemaphoreType.DMA((copies,)),
        pltpu.SemaphoreType.DMA((copies,)),
    ]
    flow, grads = pl.pallas_call(
        functools.partial(kernel, nx, nz),
        out_shape=[
            jax.ShapeDtypeStruct((2, POSITIONS), F32),
            jax.ShapeDtypeStruct((2, rows, EXP), BF16),
        ],
        in_specs=[hbm] * 8,
        out_specs=[hbm, hbm],
        scratch_shapes=scratch,
        compiler_params=pltpu.CompilerParams(
            collective_id=0, has_side_effects=True, vmem_limit_bytes=56 * 1024 * 1024
        ),
    )(
        feat_a,
        feat_b,
        flow_in_weight.T,
        flow_entry_bias.reshape(1, DEC),
        flow_out_weight,
        frame_mix,
        expand_weight,
        expand_bias.reshape(1, EXP),
    )
    flow, grads = pl.pallas_call(
        hand_out,
        out_shape=[
            jax.ShapeDtypeStruct((2, POSITIONS), F32),
            jax.ShapeDtypeStruct((2, rows, EXP), BF16),
        ],
        in_specs=[hbm, hbm],
        out_specs=[hbm, hbm],
        scratch_shapes=[
            pltpu.VMEM((2, POSITIONS), F32),
            pltpu.VMEM((2, rows, EXP), BF16),
            pltpu.SemaphoreType.DMA((5,)),
            pltpu.SemaphoreType.DMA((5,)),
        ],
    )(flow, grads)
    return (
        flow.reshape(1, 1, 2, POSITIONS),
        grads.reshape(2, 1, frames, block, EXP),
    )


def solution(mesh):
    nx = math.isqrt(mesh.shape["tm"])
    nz = mesh.shape["batch"] // 2
    return jax.shard_map(
        functools.partial(on_device, nx, nz),
        mesh=mesh,
        in_specs=(
            P("batch", "tm", None, None),
            P("batch", "tm", None, None),
            P(),
            P(),
            P(),
            P(),
            P(),
            P(),
        ),
        out_specs=(P("batch", "tm", None, None), P(None, "batch", None, "tm", None)),
        check_vma=False,
    )
```

```python
import functools
import math

import jax
import jax.numpy as jnp
from jax import lax
from jax.experimental import pallas as pl
from jax.experimental.pallas import tpu as pltpu
from jax.sharding import PartitionSpec as P

MESH = pl.DeviceIdType.MESH
F32 = jnp.float32
BF16 = jnp.bfloat16

HF = 64
WF = 64
D_FEAT = 256
EXP = 1024
HALF = EXP // 2
DEC = 128
DISP = 81
POSITIONS = HF * WF
POOLED = 256
GROUP = 4 * WF
TASK = 32 * WF
REACH = 4 * WF
NEXT_ROWS = TASK + 2 * REACH
UNROLL = 2
STRIP = 34 * WF

SCHEDULE = {
    "embed": [("send", 0, 1)],
    "first": [("send", 1, 2)],
    "second": [("send", 2, 3)],
    "third": [("send", 3, 4), ("upper", 0, 2)],
    "back z": [("upper", 2, 4), ("lower", 0, 2)],
    "back 2": [("upper", 4, 6), ("lower", 2, 4)],
    "back 1": [("upper", 6, 8), ("lower", 4, 8)],
}

NN = (((1,), (0,)), ((), ()))
NT = (((1,), (1,)), ((), ()))
TN = (((0,), (0,)), ((), ()))


def mm(a, b, dims=NN, precision=None):
    return lax.dot_general(a, b, dims, precision=precision, preferred_element_type=F32)


def iota(shape, axis):
    return lax.broadcasted_iota(jnp.int32, shape, axis)


def gelu(x):
    return 0.5 * x * (1.0 + jnp.tanh(math.sqrt(2.0 / math.pi) * (x + 0.044715 * (x * x * x))))


def one_hot(condition):
    return jnp.where(condition, 1.0, 0.0).astype(BF16)


def turn(size, kind):
    hit = (iota((size, size), 0) ^ 63) == iota((size, size), 1)
    return jnp.where(hit, 1.0, 0.0).astype(kind)


def band_weights(w_in, odd):
    shape = (5 * 128, DISP)
    row, col = iota(shape, 0), iota(shape, 1)
    lane = (row + 4) & 127
    dy = (row >> 7) * 2 + 1 - (lane >> 6) - odd
    dx = lane & 63
    hit = (dx < 9) & (dy >= 0) & (dy < 9) & (dy * 9 + dx == col)
    return (mm(one_hot(hit), w_in.astype(BF16)) * (1.0 / math.sqrt(D_FEAT))).astype(BF16)


def conv_weights(w_out_ref):
    zeros = jnp.zeros((2, DEC), F32)
    rows = []
    for kx in (2, 1, 0):
        rows += [w_out_ref[ky, kx] for ky in range(3)] + [zeros]
    rows += [jnp.zeros((8, DEC), F32)]
    return jnp.concatenate(rows, axis=0).astype(BF16)


def mixing_weights(mix, frames, block):
    size = frames * block
    spread = one_hot(lax.div(iota((size, frames), 0), block) == iota((size, frames), 1))
    same = lax.rem(iota((size, size), 0), block) == lax.rem(iota((size, size), 1), block)
    high = mix.astype(BF16)
    low = (mix - high.astype(F32)).astype(BF16)
    parts = []
    for part in (high, low):
        rows = mm(spread, part).astype(BF16)
        parts.append(jnp.where(same, mm(rows, spread, NT), 0.0).astype(BF16))
    return parts


def hidden_rows(low, high, first_ref, first_at, next_ref, next_at, band_ref, bias, hid_ref):
    x, lane = 63 - iota((WF, 128), 0), (iota((WF, 128), 1) + 4) & 63
    inside = (lane < 9) & (x + lane >= 4) & (x + lane < WF + 4)

    def group(g, carry):
        at = pl.multiple_of(g * GROUP, GROUP)
        first = first_ref[pl.ds(first_at + at, GROUP), :]
        latter = next_ref[pl.ds(next_at + at, 3 * GROUP), :]
        products = mm(first, latter, NT)
        for odd in range(2):
            pieces = []
            for i in (odd, odd + 2):
                blocks = []
                for m in range(i // 2, i // 2 + 5):
                    block = products[i * WF : (i + 1) * WF, m * 128 : (m + 1) * 128]
                    block = pltpu.roll(block, 1, 1, stride=1, stride_axis=0)
                    blocks.append(jnp.where(inside, block, 0.0).astype(BF16))
                pieces.append(jnp.concatenate(blocks, axis=1))
            skewed = jnp.concatenate(pieces, axis=0)
            hidden = gelu(mm(skewed, band_ref[odd]) + bias).astype(BF16)
            hid_ref[pl.ds(at + odd * WF, WF), :] = hidden[:WF]
            hid_ref[pl.ds(at + (odd + 2) * WF, WF), :] = hidden[WF:]
        return carry

    lax.fori_loop(low, high, group, 0, unroll=UNROLL)


def flow_rows(hid_ref, conv, base):
    taps = mm(conv, hid_ref[...], NT)
    lane = iota((8, TASK), 1) & 63
    across = (
        taps[8:16]
        + jnp.where(lane != 0, pltpu.roll(taps[0:8], 1, 1), 0.0)
        + jnp.where(lane != 63, pltpu.roll(taps[16:24], TASK - 1, 1), 0.0)
    )
    wide = TASK + 256
    across = jnp.concatenate([across, jnp.zeros((8, 256), F32)], axis=1)
    total = pltpu.roll(across, base + 64, 1)
    middle = pltpu.roll(across, base, 1) if base else across
    total = total + pltpu.roll(middle, 6, 0)
    total = total + pltpu.roll(pltpu.roll(across, (base + wide - 64) % wide, 1), 4, 0)
    blocks = [total[:, k * 128 : (k + 1) * 128] for k in range(STRIP // 128)]
    turned = mm(jnp.concatenate(blocks, axis=0), turn(128, F32), precision=lax.Precision.HIGHEST)
    return jnp.concatenate([turned[k * 8 : (k + 1) * 8] for k in range(STRIP // 128)], axis=1)


def kernel(
    nx,
    nz,
    fa_ref,
    fb_ref,
    w_in_any,
    b_in_any,
    w_out_any,
    mix_any,
    ew_any,
    eb_any,
    flow_any,
    grad_ref,
    w_in_ref,
    b_in_ref,
    w_out_ref,
    mix_ref,
    ew_ref,
    eb_ref,
    flow_ref,
    a_buf,
    b_buf,
    t_buf,
    rn_buf,
    rp_buf,
    band,
    conv,
    mixer,
    pooled,
    got,
    z_buf,
    zc_buf,
    zt_buf,
    mean0,
    mean_x,
    mean_y,
    mean1,
    mean_x2,
    mean_y2,
    mean2,
    mean_z,
    dev,
    send_1,
    recv_1,
    send_2,
    recv_2,
    send_3,
    recv_3,
    small,
    cov_z,
    cov_mid,
    cov_all,
    matrix,
    hid,
    strip_send,
    strip_recv,
    strip_own,
    grads,
    local_sem,
    view_sem,
    send_sem,
    recv_sem,
):
    frames = nx * nx
    block = POOLED // frames
    rows = frames * block
    local_rows = 2 * rows
    lb = HALF // nx
    zr = lb // nz

    batch, t = lax.axis_index("batch"), lax.axis_index("tm")
    z, core = lax.div(batch, 2), lax.rem(batch, 2)
    x, y = lax.div(t, nx), lax.rem(t, nx)
    other = 1 - core

    def around(i, d, n):
        return lax.rem(i + d, n)

    x_peers = [(batch, around(x, d, nx) * nx + y) for d in range(1, nx)]
    y_peers = [(batch, x * nx + around(y, d, nx)) for d in range(1, nx)]
    z_peers = [(around(z, d, nz) * 2 + core, t) for d in range(1, nz)]
    partner = (z * 2 + other, t)
    before = (batch, lax.rem(t + frames - 1, frames))
    after = (batch, lax.rem(t + 1, frames))

    count = [0]

    def remote(src, dst, device):
        i = count[0]
        count[0] += 1
        return pltpu.make_async_remote_copy(
            src_ref=src,
            dst_ref=dst,
            send_sem=send_sem.at[i],
            recv_sem=recv_sem.at[i],
            device_id=device,
            device_id_type=MESH,
        )

    def start(copies):
        for copy in copies:
            copy.start()
        started.extend(copies)

    def arrived(copies):
        for copy in copies:
            copy.wait_recv()

    started = []

    barrier = pltpu.get_barrier_semaphore()
    for device in z_peers + [partner]:
        pl.semaphore_signal(barrier, inc=1, device_id=device, device_id_type=MESH)

    def greet(d, carry):
        for c in range(2):
            device = (z * 2 + c, around(t, d, frames))
            pl.semaphore_signal(barrier, inc=1, device_id=device, device_id_type=MESH)
        return carry

    lax.fori_loop(1, frames, greet, 0)
    quarter = POSITIONS // 4
    load_views = []
    for k in range(4):
        part = pl.ds(k * quarter, quarter)
        load_views += [
            pltpu.make_async_copy(
                fa_ref.at[0, 0, part], a_buf.at[pl.ds(REACH + k * quarter, quarter)], view_sem.at[k]
            ),
            pltpu.make_async_copy(fb_ref.at[0, 0, part], b_buf.at[part], view_sem.at[4 + k]),
        ]
    load_mix = pltpu.make_async_copy(mix_any, mix_ref, local_sem.at[4])
    load_mix.start()
    for load in load_views:
        load.start()
    loads = []
    for i, (source, target) in enumerate(
        [(w_in_any, w_in_ref), (b_in_any, b_in_ref), (w_out_any, w_out_ref), (ew_any, ew_ref), (eb_any, eb_ref)]
    ):
        loads.append(pltpu.make_async_copy(source, target, local_sem.at[5 + i]))
        loads[i].start()

    a_buf[pl.ds(0, REACH), :] = jnp.zeros((REACH, D_FEAT), BF16)
    rn_buf[pl.ds(TASK + REACH, REACH), :] = jnp.zeros((REACH, D_FEAT), BF16)

    @pl.when(t == frames - 1)
    def _():
        rn_buf[pl.ds(0, TASK + REACH), :] = jnp.zeros((TASK + REACH, D_FEAT), BF16)

    @pl.when(t == 0)
    def _():
        rp_buf[...] = jnp.zeros((TASK, D_FEAT), BF16)

    span = POSITIONS // frames
    prow, pcol = iota((block, span), 0), iota((block, span), 1)
    pooled_at = lax.div(pcol, GROUP) * 16 + lax.div(pcol & 63, 4)
    pool = one_hot(pooled_at == prow)

    def pool_block(k, carry):
        at = pl.multiple_of(k * span, span)
        from_a = mm(pool, a_buf[pl.ds(REACH + at, span), :]) * (1.0 / 16.0)
        pooled[k, 0] = from_a.astype(BF16)
        from_b = mm(pool, b_buf[pl.ds(at, span), :]) * (1.0 / 16.0)
        pooled[k, 1] = from_b.astype(BF16)
        return carry

    for k in range(4):
        load_views[2 * k].wait()
        load_views[2 * k + 1].wait()
        lax.fori_loop(k * frames // 4, (k + 1) * frames // 4, pool_block, 0, unroll=True)
    pl.semaphore_wait(barrier, nz - 1 + 1 + 2 * (frames - 1))

    exchange = []
    for d in range(frames):
        to = around(t, d, frames)
        for view, device in ((core, (batch, to)), (other, (z * 2 + other, to))):
            if d > 0 or view is other:
                exchange.append(remote(pooled.at[to, view], got.at[core, t], device))
    start(exchange)

    turner = turn(GROUP, BF16)

    def turn_group(k, carry):
        at = pl.multiple_of(k * GROUP, GROUP)
        turned = mm(turner, a_buf[pl.ds(REACH + at, GROUP), :])
        t_buf[pl.ds(at, GROUP), :] = turned.astype(BF16)
        return carry

    lax.fori_loop(0, TASK // GROUP, turn_group, 0, unroll=4)

    to_after, to_before = [], []
    for c in range(4):
        at, size = c * 8 * WF, 8 * WF
        to_after.append(remote(t_buf.at[pl.ds(at, size)], rp_buf.at[pl.ds(at, size)], after))
        at, size = c * 8 * WF, (12 if c == 3 else 8) * WF
        to_before.append(remote(a_buf.at[pl.ds(TASK + at, size)], rn_buf.at[pl.ds(at, size)], before))

    def not_first(action):
        pl.when(t > 0)(action)

    def not_last(action):
        pl.when(t < frames - 1)(action)

    ready = set()
    strips = []

    def await_part(view, c):
        if (view, c) not in ready:
            ready.add((view, c))
            if view == 0:
                not_first(to_after[c].wait_recv)
            else:
                not_last(to_before[c].wait_recv)

    def meanwhile(point):
        for kind, low, high in SCHEDULE.get(point, ()):
            if kind == "send":
                for c in range(low, high):
                    not_first(to_before[c].start)
                    not_last(to_after[c].start)
            elif kind == "upper":
                for c in range((high + 1) // 2):
                    await_part(0, c)
                hidden_rows(low, high, rp_buf, 0, a_buf, 0, band, bias, hid.at[0])
                if high == TASK // GROUP:
                    strip_send[...] = flow_rows(hid.at[0], conv[...], 0)
                    strips.append(remote(strip_send, strip_recv, before))
                    start(strips)
            else:
                for c in range(min(3, (high + 1) // 2) + 1):
                    await_part(1, c)
                hidden_rows(low, high, t_buf, TASK, rn_buf, 0, band, bias, hid.at[1])
                if high == TASK // GROUP:
                    strip_own[...] = flow_rows(hid.at[1], conv[...], 128)

    meanwhile("exchange")
    got[core, t] = pooled[t, core]
    load_mix.wait()
    for load in loads:
        load.wait()
    bias = b_in_ref[...]
    mixer[0], mixer[1] = mixing_weights(mix_ref[...], frames, block)
    lax.fori_loop(TASK // GROUP, 2 * (TASK // GROUP), turn_group, 0, unroll=4)
    band[0] = band_weights(w_in_ref[...], 0)
    band[1] = band_weights(w_in_ref[...], 1)
    conv[...] = conv_weights(w_out_ref)
    arrived(exchange)
    meanwhile("embed")

    total = [jnp.zeros((1, 256), F32) for _ in range(EXP // 256)]
    for clip in range(2):
        features = got[clip].reshape(rows, D_FEAT)
        mixed = (mm(mixer[0], features) + mm(mixer[1], features)).astype(BF16)
        for k in range(EXP // 256):
            cols = pl.ds(k * 256, 256)
            value = gelu(mm(mixed, ew_ref[:, cols]) + eb_ref[:, cols]).astype(BF16)
            z_buf[pl.ds(clip * rows, rows), cols] = value
            total[k] = total[k] + jnp.sum(value.astype(F32), axis=0, keepdims=True)
    mean = jnp.concatenate(total, axis=1) / local_rows
    mean0[0] = mean
    share_x = [remote(mean0.at[0], mean_x.at[d - 1], x_peers[d - 1]) for d in range(1, nx)]
    share_y = [remote(mean0.at[0], mean_y.at[d - 1], y_peers[d - 1]) for d in range(1, nx)]
    start(share_x)
    start(share_y)

    def center(k, carry):
        part = pl.ds(pl.multiple_of(k * 64, 64), 64)
        zc_buf[part, :] = (z_buf[part, :].astype(F32) - mean).astype(BF16)
        return carry

    lax.fori_loop(0, local_rows // 64, center, 0)
    def transpose_columns(blocks):
        for k in blocks:
            zt_buf[pl.ds(k * 256, 256), :] = zc_buf[:, pl.ds(k * 256, 256)].T

    transpose_columns(range(HALF // 256))
    left, right = pl.ds(0, HALF), pl.ds(HALF, HALF)

    for k in range(HALF // 256):
        cols = pl.ds(HALF + k * 256, 256)
        cross = mm(zt_buf[left, :], zc_buf[:, cols]).astype(BF16)
        for j in range(256 // lb):
            send_1[0, k * (256 // lb) + j] = cross[:, j * lb : (j + 1) * lb]
    first_x = [
        remote(send_1.at[0, around(x, d, nx)], recv_1.at[0, d - 1], x_peers[d - 1])
        for d in range(1, nx)
    ]
    start(first_x)
    transpose_columns(range(HALF // 256, EXP // 256))
    row_at, col_at = iota((HALF, 256), 0), iota((HALF, 256), 1)
    for k in range(HALF // 256):
        in_left = mm(zt_buf[left, :], zc_buf[:, pl.ds(k * 256, 256)])
        in_right = mm(zt_buf[right, :], zc_buf[:, pl.ds(HALF + k * 256, 256)])
        ahead = col_at + k * 256 - row_at
        both = jnp.where(ahead > 0, in_left, jnp.where(ahead < 0, in_right, 0.0)).astype(BF16)
        for j in range(256 // lb):
            send_1[1, k * (256 // lb) + j] = both[:, j * lb : (j + 1) * lb]
    first_y = [
        remote(send_1.at[1, around(y, d, nx)], recv_1.at[1, d - 1], y_peers[d - 1])
        for d in range(1, nx)
    ]
    start(first_y)
    meanwhile("first")

    def combine(own, parts, n):
        center = own
        for i in range(n - 1):
            center = center + parts[i]
        center = center / n
        lines = [own - center] + [parts[i] - center for i in range(n - 1)]
        lines += [jnp.zeros_like(own)] * (8 - n)
        dev[...] = jnp.concatenate(lines, axis=0)
        return center

    def outer(first_at, height, second_at):
        return mm(
            dev[:, pl.ds(first_at, height)],
            dev[:, pl.ds(second_at, lb)],
            TN,
            precision=lax.Precision.HIGHEST,
        )

    def triangles(first_at, height, block_at, inner_at):
        in_left = outer(first_at, height, block_at)
        in_right = outer(HALF + first_at, height, HALF + block_at)
        ahead = (block_at + iota((height, lb), 1)) - (inner_at + iota((height, lb), 0))
        return jnp.where(ahead > 0, in_left, jnp.where(ahead < 0, in_right, 0.0))

    x_at, y_at = pl.multiple_of(x * lb, lb), pl.multiple_of(y * lb, lb)

    arrived(share_x)
    center_x = combine(mean0[0], mean_x, nx)
    mean1[0] = center_x
    carry_x = [remote(mean1.at[0], mean_x2.at[d - 1], y_peers[d - 1]) for d in range(1, nx)]
    start(carry_x)
    part = local_rows * outer(0, HALF, HALF + x_at)
    arrived(first_x)
    part = part + send_1[0, x].astype(F32)
    for i in range(nx - 1):
        part = part + recv_1[0, i].astype(F32)
    send_2[0] = part.astype(BF16)
    second_x = [
        remote(
            send_2.at[0, pl.ds(pl.multiple_of(around(y, d, nx) * lb, lb), lb)],
            recv_2.at[0, d - 1],
            y_peers[d - 1],
        )
        for d in range(1, nx)
    ]
    start(second_x)

    arrived(share_y)
    center_y = combine(mean0[0], mean_y, nx)
    mean1[1] = center_y
    carry_y = [remote(mean1.at[1], mean_y2.at[d - 1], x_peers[d - 1]) for d in range(1, nx)]
    start(carry_y)
    part = local_rows * triangles(0, HALF, y_at, 0)
    arrived(first_y)
    part = part + send_1[1, y].astype(F32)
    for i in range(nx - 1):
        part = part + recv_1[1, i].astype(F32)
    send_2[1] = part.astype(BF16)
    second_y = [
        remote(
            send_2.at[1, pl.ds(pl.multiple_of(around(x, d, nx) * lb, lb), lb)],
            recv_2.at[1, d - 1],
            x_peers[d - 1],
        )
        for d in range(1, nx)
    ]
    start(second_y)
    meanwhile("second")

    arrived(carry_x)
    center_xy = combine(mean1[0], mean_x2, nx)
    mean2[0] = center_xy
    carry_z = [remote(mean2.at[0], mean_z.at[d - 1], z_peers[d - 1]) for d in range(1, nz)]
    start(carry_z)
    part = (local_rows * nx) * outer(y_at, lb, HALF + x_at)
    arrived(second_x)
    part = part + send_2[0, pl.ds(y_at, lb)].astype(F32)
    for i in range(nx - 1):
        part = part + recv_2[0, i].astype(F32)
    send_3[0] = part.astype(BF16)

    arrived(carry_y)
    combine(mean1[1], mean_y2, nx)
    part = (local_rows * nx) * triangles(x_at, lb, y_at, x_at)
    arrived(second_y)
    part = part + send_2[1, pl.ds(x_at, lb)].astype(F32)
    for i in range(nx - 1):
        part = part + recv_2[1, i].astype(F32)
    send_3[1] = part.astype(BF16)

    def z_rows(i):
        return pl.ds(pl.multiple_of(i * zr, zr), zr)

    third = [
        remote(send_3.at[:, z_rows(around(z, d, nz))], recv_3.at[d - 1], z_peers[d - 1])
        for d in range(1, nz)
    ]
    start(third)
    meanwhile("third")
    arrived(carry_z)
    mean = combine(mean2[0], mean_z, nz)
    group_rows = local_rows * frames
    small[0] = group_rows * outer(y_at, lb, HALF + x_at)
    small[1] = group_rows * triangles(x_at, lb, y_at, x_at)
    arrived(third)
    part = small[:, z_rows(z), :] + send_3[:, z_rows(z), :].astype(F32)
    for i in range(nz - 1):
        part = part + recv_3[i].astype(F32)
    scale = 1.0 / (group_rows * nz - 1) / math.sqrt(EXP)
    cov_z[:, z_rows(z), :] = (part * scale).astype(BF16)

    back_z = [
        remote(cov_z.at[:, z_rows(z)], cov_z.at[:, z_rows(z)], z_peers[d - 1])
        for d in range(1, nz)
    ]
    start(back_z)

    def center_all(k, carry):
        part = pl.ds(pl.multiple_of(k * 64, 64), 64)
        zc_buf[part, :] = (z_buf[part, :].astype(F32) - mean).astype(BF16)
        return carry

    lax.fori_loop(0, local_rows // 64, center_all, 0)
    meanwhile("back z")
    arrived(back_z)
    y_rows, x_rows = pl.ds(y_at, lb), pl.ds(x_at, lb)
    back_2 = [
        remote(cov_z.at[0], cov_mid.at[0, y_rows], y_peers[d - 1]) for d in range(1, nx)
    ] + [remote(cov_z.at[1], cov_mid.at[1, x_rows], x_peers[d - 1]) for d in range(1, nx)]
    start(back_2)
    cov_mid[0, y_rows] = cov_z[0]
    cov_mid[1, x_rows] = cov_z[1]
    meanwhile("back 2")
    arrived(back_2)
    back_1 = [
        remote(cov_mid.at[0], cov_all.at[0, x], x_peers[d - 1]) for d in range(1, nx)
    ] + [remote(cov_mid.at[1], cov_all.at[1, y], y_peers[d - 1]) for d in range(1, nx)]
    start(back_1)
    cov_all[0, x] = cov_mid[0]
    cov_all[1, y] = cov_mid[1]

    meanwhile("back 1")

    pieces = HALF // lb
    arrived(back_1[: nx - 1])
    cross = jnp.concatenate([cov_all[0, k] for k in range(pieces)], axis=1)
    matrix[left, right] = cross
    matrix[right, left] = cross.T
    arrived(back_1[nx - 1 :])
    both = jnp.concatenate([cov_all[1, k] for k in range(pieces)], axis=1)
    turned = both.T
    ahead = iota((HALF, HALF), 1) - iota((HALF, HALF), 0)
    matrix[left, left] = jnp.where(ahead > 0, both, turned)
    matrix[right, right] = jnp.where(ahead < 0, both, turned)

    def gradient(slot, clip):
        lines = pl.ds(pl.multiple_of(clip * rows, rows), rows)
        for k in range(2):
            for j in range(2):
                cols = pl.ds(k * HALF + j * 256, 256)
                grads[slot, :, cols] = mm(zc_buf[lines, :], matrix[:, cols]).astype(BF16)
            cols = pl.ds(k * HALF, HALF)
            if slot == 0:
                copy = remote(grads.at[0, :, cols], grad_ref.at[core, :, cols], partner)
                start([copy])
            else:
                copy = pltpu.make_async_copy(
                    grads.at[1, :, cols], grad_ref.at[core, :, cols], local_sem.at[2 + k]
                )
                copy.start()
            results.append(copy)

    results = []
    gradient(0, other)
    gradient(1, core)

    arrived(strips)
    edge = STRIP - 256
    top, bottom = strip_recv[...], strip_own[...]
    flow_ref[:, 0:edge] = top[0:2, :edge]
    flow_ref[:, edge:STRIP] = top[0:2, edge:] + bottom[0:2, :256]
    flow_ref[:, STRIP:] = bottom[0:2, 256:]
    store = pltpu.make_async_copy(flow_ref, flow_any, local_sem.at[10])
    store.start()

    for copy in results:
        copy.wait_recv()
    store.wait()
    for c in range(4):
        not_first(to_before[c].wait_send)
        not_last(to_after[c].wait_send)
    for copy in started:
        copy.wait_send()


def hand_out(flow_in, grads_in, flow_out, grads_out, flow_held, held, in_sem, out_sem):
    loads, stores = [], []
    for k in range(4):
        part = (k // 2, pl.ds((k % 2) * 128, 128))
        loads.append(pltpu.make_async_copy(grads_in.at[part], held.at[part], in_sem.at[k]))
        stores.append(pltpu.make_async_copy(held.at[part], grads_out.at[part], out_sem.at[k]))
    loads.append(pltpu.make_async_copy(flow_in, flow_held, in_sem.at[4]))
    stores.append(pltpu.make_async_copy(flow_held, flow_out, out_sem.at[4]))
    for load in loads:
        load.start()
    for load, store in zip(loads, stores):
        load.wait()
        store.start()
    for store in stores:
        store.wait()


def on_device(
    nx,
    nz,
    feat_a,
    feat_b,
    flow_in_weight,
    flow_entry_bias,
    flow_out_weight,
    frame_mix,
    expand_weight,
    expand_bias,
):
    frames = nx * nx
    block = POOLED // frames
    rows = frames * block
    lb = HALF // nx
    zr = lb // nz
    copies = 2 * frames - 1 + 8 + 12 * (nx - 1) + 3 * (nz - 1) + 3
    hbm = pl.BlockSpec(memory_space=pl.ANY)
    scratch = [
        pltpu.VMEM((DISP, DEC), F32),
        pltpu.VMEM((1, DEC), F32),
        pltpu.VMEM((3, 3, 2, DEC), F32),
        pltpu.VMEM((frames, frames), F32),
        pltpu.VMEM((D_FEAT, EXP), BF16),
        pltpu.VMEM((1, EXP), F32),
        pltpu.VMEM((2, POSITIONS), F32),
        pltpu.VMEM((REACH + POSITIONS, D_FEAT), BF16),
        pltpu.VMEM((POSITIONS, D_FEAT), BF16),
        pltpu.VMEM((POSITIONS, D_FEAT), BF16),
        pltpu.VMEM((NEXT_ROWS, D_FEAT), BF16),
        pltpu.VMEM((TASK, D_FEAT), BF16),
        pltpu.VMEM((2, 640, DEC), BF16),
        pltpu.VMEM((32, DEC), BF16),
        pltpu.VMEM((2, rows, rows), BF16),
        pltpu.VMEM((frames, 2, block, D_FEAT), BF16),
        pltpu.VMEM((2, frames, block, D_FEAT), BF16),
        pltpu.VMEM((2 * rows, EXP), BF16),
        pltpu.VMEM((2 * rows, EXP), BF16),
        pltpu.VMEM((EXP, 2 * rows), BF16),
        pltpu.VMEM((1, 1, EXP), F32),
        pltpu.VMEM((nx - 1, 1, EXP), F32),
        pltpu.VMEM((nx - 1, 1, EXP), F32),
        pltpu.VMEM((2, 1, EXP), F32),
        pltpu.VMEM((nx - 1, 1, EXP), F32),
        pltpu.VMEM((nx - 1, 1, EXP), F32),
        pltpu.VMEM((1, 1, EXP), F32),
        pltpu.VMEM((nz - 1, 1, EXP), F32),
        pltpu.VMEM((8, EXP), F32),
        pltpu.VMEM((2, nx, HALF, lb), BF16),
        pltpu.VMEM((2, nx - 1, HALF, lb), BF16),
        pltpu.VMEM((2, HALF, lb), BF16),
        pltpu.VMEM((2, nx - 1, lb, lb), BF16),
        pltpu.VMEM((2, lb, lb), BF16),
        pltpu.VMEM((nz - 1, 2, zr, lb), BF16),
        pltpu.VMEM((2, lb, lb), F32),
        pltpu.VMEM((2, lb, lb), BF16),
        pltpu.VMEM((2, HALF, lb), BF16),
        pltpu.VMEM((2, nx, HALF, lb), BF16),
        pltpu.VMEM((EXP, EXP), BF16),
        pltpu.VMEM((2, TASK, DEC), BF16),
        pltpu.VMEM((8, STRIP), F32),
        pltpu.VMEM((8, STRIP), F32),
        pltpu.VMEM((8, STRIP), F32),
        pltpu.VMEM((2, rows, EXP), BF16),
        pltpu.SemaphoreType.DMA((11,)),
        pltpu.SemaphoreType.DMA((8,)),
        pltpu.SemaphoreType.DMA((copies,)),
        pltpu.SemaphoreType.DMA((copies,)),
    ]
    flow, grads = pl.pallas_call(
        functools.partial(kernel, nx, nz),
        out_shape=[
            jax.ShapeDtypeStruct((2, POSITIONS), F32),
            jax.ShapeDtypeStruct((2, rows, EXP), BF16),
        ],
        in_specs=[hbm] * 8,
        out_specs=[hbm, hbm],
        scratch_shapes=scratch,
        compiler_params=pltpu.CompilerParams(
            collective_id=0, has_side_effects=True, vmem_limit_bytes=56 * 1024 * 1024
        ),
    )(
        feat_a,
        feat_b,
        flow_in_weight.T,
        flow_entry_bias.reshape(1, DEC),
        flow_out_weight,
        frame_mix,
        expand_weight,
        expand_bias.reshape(1, EXP),
    )
    flow, grads = pl.pallas_call(
        hand_out,
        out_shape=[
            jax.ShapeDtypeStruct((2, POSITIONS), F32),
            jax.ShapeDtypeStruct((2, rows, EXP), BF16),
        ],
        in_specs=[hbm, hbm],
        out_specs=[hbm, hbm],
        scratch_shapes=[
            pltpu.VMEM((2, POSITIONS), F32),
            pltpu.VMEM((2, rows, EXP), BF16),
            pltpu.SemaphoreType.DMA((5,)),
            pltpu.SemaphoreType.DMA((5,)),
        ],
    )(flow, grads)
    return (
        flow.reshape(1, 1, 2, POSITIONS),
        grads.reshape(2, 1, frames, block, EXP),
    )


def solution(mesh):
    nx = math.isqrt(mesh.shape["tm"])
    nz = mesh.shape["batch"] // 2
    return jax.shard_map(
        functools.partial(on_device, nx, nz),
        mesh=mesh,
        in_specs=(
            P("batch", "tm", None, None),
            P("batch", "tm", None, None),
            P(),
            P(),
            P(),
            P(),
            P(),
            P(),
        ),
        out_specs=(P("batch", "tm", None, None), P(None, "batch", None, "tm", None)),
        check_vma=False,
    )
```

```python
import functools
import math

import jax
import jax.numpy as jnp
from jax import lax
from jax.experimental import pallas as pl
from jax.experimental.pallas import tpu as pltpu
from jax.sharding import PartitionSpec as P

MESH = pl.DeviceIdType.MESH
F32 = jnp.float32
BF16 = jnp.bfloat16

HF = 64
WF = 64
D_FEAT = 256
EXP = 1024
HALF = EXP // 2
DEC = 128
DISP = 81
POSITIONS = HF * WF
POOLED = 256
GROUP = 4 * WF
TASK = 32 * WF
REACH = 4 * WF
NEXT_ROWS = TASK + 2 * REACH
UNROLL = 2
PARTS = 4
STRIP = 34 * WF

SCHEDULE = {
    "embed": [("send", 0, 1)],
    "first": [("send", 1, 2)],
    "second": [("send", 2, 3)],
    "third": [("send", 3, 4), ("upper", 0, 2)],
    "back z": [("upper", 2, 4), ("lower", 0, 2)],
    "back 2": [("upper", 4, 6), ("lower", 2, 4)],
    "back 1": [("upper", 6, 8), ("lower", 4, 8)],
}

NN = (((1,), (0,)), ((), ()))
NT = (((1,), (1,)), ((), ()))
TN = (((0,), (0,)), ((), ()))


def mm(a, b, dims=NN, precision=None):
    return lax.dot_general(a, b, dims, precision=precision, preferred_element_type=F32)


def iota(shape, axis):
    return lax.broadcasted_iota(jnp.int32, shape, axis)


def gelu(x):
    return 0.5 * x * (1.0 + jnp.tanh(math.sqrt(2.0 / math.pi) * (x + 0.044715 * (x * x * x))))


def one_hot(condition):
    return jnp.where(condition, 1.0, 0.0).astype(BF16)


def turn(size, kind):
    hit = (iota((size, size), 0) ^ 63) == iota((size, size), 1)
    return jnp.where(hit, 1.0, 0.0).astype(kind)


def band_weights(w_in, odd):
    shape = (5 * 128, DISP)
    row, col = iota(shape, 0), iota(shape, 1)
    lane = (row + 4) & 127
    dy = (row >> 7) * 2 + 1 - (lane >> 6) - odd
    dx = lane & 63
    hit = (dx < 9) & (dy >= 0) & (dy < 9) & (dy * 9 + dx == col)
    return (mm(one_hot(hit), w_in.astype(BF16)) * (1.0 / math.sqrt(D_FEAT))).astype(BF16)


def conv_weights(w_out_ref):
    zeros = jnp.zeros((2, DEC), F32)
    rows = []
    for kx in (2, 1, 0):
        rows += [w_out_ref[ky, kx] for ky in range(3)] + [zeros]
    rows += [jnp.zeros((8, DEC), F32)]
    return jnp.concatenate(rows, axis=0).astype(BF16)


def mixing_weights(mix, frames, block):
    size = frames * block
    spread = one_hot(lax.div(iota((size, frames), 0), block) == iota((size, frames), 1))
    same = lax.rem(iota((size, size), 0), block) == lax.rem(iota((size, size), 1), block)
    high = mix.astype(BF16)
    low = (mix - high.astype(F32)).astype(BF16)
    parts = []
    for part in (high, low):
        rows = mm(spread, part).astype(BF16)
        parts.append(jnp.where(same, mm(rows, spread, NT), 0.0).astype(BF16))
    return parts


def hidden_rows(low, high, first_ref, first_at, next_ref, next_at, band_ref, bias, hid_ref):
    x, lane = 63 - iota((WF, 128), 0), (iota((WF, 128), 1) + 4) & 63
    inside = (lane < 9) & (x + lane >= 4) & (x + lane < WF + 4)

    def group(g, carry):
        at = pl.multiple_of(g * GROUP, GROUP)
        first = first_ref[pl.ds(first_at + at, GROUP), :]
        latter = next_ref[pl.ds(next_at + at, 3 * GROUP), :]
        products = mm(first, latter, NT)
        for odd in range(2):
            pieces = []
            for i in (odd, odd + 2):
                blocks = []
                for m in range(i // 2, i // 2 + 5):
                    block = products[i * WF : (i + 1) * WF, m * 128 : (m + 1) * 128]
                    block = pltpu.roll(block, 1, 1, stride=1, stride_axis=0)
                    blocks.append(jnp.where(inside, block, 0.0).astype(BF16))
                pieces.append(jnp.concatenate(blocks, axis=1))
            skewed = jnp.concatenate(pieces, axis=0)
            hidden = gelu(mm(skewed, band_ref[odd]) + bias).astype(BF16)
            hid_ref[pl.ds(at + odd * WF, WF), :] = hidden[:WF]
            hid_ref[pl.ds(at + (odd + 2) * WF, WF), :] = hidden[WF:]
        return carry

    lax.fori_loop(low, high, group, 0, unroll=UNROLL)


def flow_rows(hid_ref, conv, base):
    taps = mm(conv, hid_ref[...], NT)
    lane = iota((8, TASK), 1) & 63
    across = (
        taps[8:16]
        + jnp.where(lane != 0, pltpu.roll(taps[0:8], 1, 1), 0.0)
        + jnp.where(lane != 63, pltpu.roll(taps[16:24], TASK - 1, 1), 0.0)
    )
    wide = TASK + 256
    across = jnp.concatenate([across, jnp.zeros((8, 256), F32)], axis=1)
    total = pltpu.roll(across, base + 64, 1)
    middle = pltpu.roll(across, base, 1) if base else across
    total = total + pltpu.roll(middle, 6, 0)
    total = total + pltpu.roll(pltpu.roll(across, (base + wide - 64) % wide, 1), 4, 0)
    blocks = [total[:, k * 128 : (k + 1) * 128] for k in range(STRIP // 128)]
    turned = mm(jnp.concatenate(blocks, axis=0), turn(128, F32), precision=lax.Precision.HIGHEST)
    return jnp.concatenate([turned[k * 8 : (k + 1) * 8] for k in range(STRIP // 128)], axis=1)


def kernel(
    nx,
    nz,
    fa_ref,
    fb_ref,
    w_in_any,
    b_in_any,
    w_out_any,
    mix_any,
    ew_any,
    eb_any,
    flow_any,
    grad_ref,
    w_in_ref,
    b_in_ref,
    w_out_ref,
    mix_ref,
    ew_ref,
    eb_ref,
    flow_ref,
    a_buf,
    b_buf,
    t_buf,
    rn_buf,
    rp_buf,
    band,
    conv,
    mixer,
    pooled,
    got,
    z_buf,
    zc_buf,
    zt_buf,
    mean0,
    mean_x,
    mean_y,
    mean1,
    mean_x2,
    mean_y2,
    mean2,
    mean_z,
    dev,
    send_1,
    recv_1,
    send_2,
    recv_2,
    send_3,
    recv_3,
    small,
    cov_z,
    cov_mid,
    cov_all,
    matrix,
    hid,
    strip_send,
    strip_recv,
    strip_own,
    grads,
    local_sem,
    view_sem,
    send_sem,
    recv_sem,
):
    frames = nx * nx
    block = POOLED // frames
    rows = frames * block
    local_rows = 2 * rows
    lb = HALF // nx
    zr = lb // nz

    batch, t = lax.axis_index("batch"), lax.axis_index("tm")
    z, core = lax.div(batch, 2), lax.rem(batch, 2)
    x, y = lax.div(t, nx), lax.rem(t, nx)
    other = 1 - core

    def around(i, d, n):
        return lax.rem(i + d, n)

    x_peers = [(batch, around(x, d, nx) * nx + y) for d in range(1, nx)]
    y_peers = [(batch, x * nx + around(y, d, nx)) for d in range(1, nx)]
    z_peers = [(around(z, d, nz) * 2 + core, t) for d in range(1, nz)]
    partner = (z * 2 + other, t)
    before = (batch, lax.rem(t + frames - 1, frames))
    after = (batch, lax.rem(t + 1, frames))

    count = [0]

    def remote(src, dst, device):
        i = count[0]
        count[0] += 1
        return pltpu.make_async_remote_copy(
            src_ref=src,
            dst_ref=dst,
            send_sem=send_sem.at[i],
            recv_sem=recv_sem.at[i],
            device_id=device,
            device_id_type=MESH,
        )

    def start(copies):
        for copy in copies:
            copy.start()
        started.extend(copies)

    def arrived(copies):
        for copy in copies:
            copy.wait_recv()

    started = []

    quarter = POSITIONS // 4
    load_views = []
    for k in range(4):
        part = pl.ds(k * quarter, quarter)
        load_views += [
            pltpu.make_async_copy(
                fa_ref.at[0, 0, part], a_buf.at[pl.ds(REACH + k * quarter, quarter)], view_sem.at[k]
            ),
            pltpu.make_async_copy(fb_ref.at[0, 0, part], b_buf.at[part], view_sem.at[4 + k]),
        ]
    load_mix = pltpu.make_async_copy(mix_any, mix_ref, local_sem.at[4])
    load_mix.start()
    for load in load_views:
        load.start()
    loads = []
    for i, (source, target) in enumerate(
        [(w_in_any, w_in_ref), (b_in_any, b_in_ref), (w_out_any, w_out_ref), (ew_any, ew_ref), (eb_any, eb_ref)]
    ):
        loads.append(pltpu.make_async_copy(source, target, local_sem.at[5 + i]))
        loads[i].start()

    barrier = pltpu.get_barrier_semaphore()
    for device in z_peers + [partner]:
        pl.semaphore_signal(barrier, inc=1, device_id=device, device_id_type=MESH)

    def greet(d, carry):
        for c in range(2):
            device = (z * 2 + c, around(t, d, frames))
            pl.semaphore_signal(barrier, inc=1, device_id=device, device_id_type=MESH)
        return carry

    lax.fori_loop(1, frames, greet, 0)
    span = POSITIONS // frames
    prow, pcol = iota((block, span), 0), iota((block, span), 1)
    pooled_at = lax.div(pcol, GROUP) * 16 + lax.div(pcol & 63, 4)
    pool = one_hot(pooled_at == prow)

    def pool_block(k, carry):
        at = pl.multiple_of(k * span, span)
        from_a = mm(pool, a_buf[pl.ds(REACH + at, span), :]) * (1.0 / 16.0)
        pooled[k, 0] = from_a.astype(BF16)
        from_b = mm(pool, b_buf[pl.ds(at, span), :]) * (1.0 / 16.0)
        pooled[k, 1] = from_b.astype(BF16)
        return carry

    for k in range(4):
        load_views[2 * k].wait()
        load_views[2 * k + 1].wait()
        lax.fori_loop(k * frames // 4, (k + 1) * frames // 4, pool_block, 0, unroll=True)
    pl.semaphore_wait(barrier, nz - 1 + 1 + 2 * (frames - 1))

    exchange = []
    for d in range(frames):
        to = around(t, d, frames)
        for view, device in ((core, (batch, to)), (other, (z * 2 + other, to))):
            if d > 0 or view is other:
                exchange.append(remote(pooled.at[to, view], got.at[core, t], device))
    start(exchange)

    turner = turn(GROUP, BF16)

    def turn_group(k, carry):
        at = pl.multiple_of(k * GROUP, GROUP)
        turned = mm(turner, a_buf[pl.ds(REACH + at, GROUP), :])
        t_buf[pl.ds(at, GROUP), :] = turned.astype(BF16)
        return carry

    lax.fori_loop(0, TASK // GROUP, turn_group, 0, unroll=4)

    to_after, to_before = [], []
    for c in range(PARTS):
        at, size = c * 8 * WF, 8 * WF
        to_after.append(remote(t_buf.at[pl.ds(at, size)], rp_buf.at[pl.ds(at, size)], after))
        at, size = c * 8 * WF, (12 if c == PARTS - 1 else 8) * WF
        to_before.append(remote(a_buf.at[pl.ds(TASK + at, size)], rn_buf.at[pl.ds(at, size)], before))

    def not_first(action):
        pl.when(t > 0)(action)

    def not_last(action):
        pl.when(t < frames - 1)(action)

    ready = set()
    strips = []

    def await_part(view, c):
        if (view, c) not in ready:
            ready.add((view, c))
            if view == 0:
                not_first(to_after[c].wait_recv)
            else:
                not_last(to_before[c].wait_recv)

    def meanwhile(point):
        for kind, low, high in SCHEDULE.get(point, ()):
            if kind == "send":
                for c in range(low, high):
                    not_first(to_before[c].start)
                    not_last(to_after[c].start)
            elif kind == "upper":
                for c in range((high + 1) // 2):
                    await_part(0, c)
                hidden_rows(low, high, rp_buf, 0, a_buf, 0, band, bias, hid.at[0])
                if high == TASK // GROUP:
                    strip_send[...] = flow_rows(hid.at[0], conv[...], 0)
                    strips.append(remote(strip_send, strip_recv, before))
                    start(strips)
            else:
                for c in range(min(PARTS, (high + 3) // 2)):
                    await_part(1, c)
                hidden_rows(low, high, t_buf, TASK, rn_buf, 0, band, bias, hid.at[1])
                if high == TASK // GROUP:
                    strip_own[...] = flow_rows(hid.at[1], conv[...], 128)

    a_buf[pl.ds(0, REACH), :] = jnp.zeros((REACH, D_FEAT), BF16)
    rn_buf[pl.ds(TASK + REACH, REACH), :] = jnp.zeros((REACH, D_FEAT), BF16)

    @pl.when(t == frames - 1)
    def _():
        rn_buf[pl.ds(0, TASK + REACH), :] = jnp.zeros((TASK + REACH, D_FEAT), BF16)

    @pl.when(t == 0)
    def _():
        rp_buf[...] = jnp.zeros((TASK, D_FEAT), BF16)

    meanwhile("exchange")
    got[core, t] = pooled[t, core]
    load_mix.wait()
    for load in loads:
        load.wait()
    bias = b_in_ref[...]
    mixer[0], mixer[1] = mixing_weights(mix_ref[...], frames, block)
    lax.fori_loop(TASK // GROUP, 2 * (TASK // GROUP), turn_group, 0, unroll=4)
    band[0] = band_weights(w_in_ref[...], 0)
    band[1] = band_weights(w_in_ref[...], 1)
    conv[...] = conv_weights(w_out_ref)
    arrived(exchange)
    meanwhile("embed")

    total = [jnp.zeros((1, 256), F32) for _ in range(EXP // 256)]
    for clip in range(2):
        features = got[clip].reshape(rows, D_FEAT)
        mixed = (mm(mixer[0], features) + mm(mixer[1], features)).astype(BF16)
        for k in range(EXP // 256):
            cols = pl.ds(k * 256, 256)
            value = gelu(mm(mixed, ew_ref[:, cols]) + eb_ref[:, cols]).astype(BF16)
            z_buf[pl.ds(clip * rows, rows), cols] = value
            total[k] = total[k] + jnp.sum(value.astype(F32), axis=0, keepdims=True)
    mean = jnp.concatenate(total, axis=1) / local_rows
    mean0[0] = mean
    share_x = [remote(mean0.at[0], mean_x.at[d - 1], x_peers[d - 1]) for d in range(1, nx)]
    share_y = [remote(mean0.at[0], mean_y.at[d - 1], y_peers[d - 1]) for d in range(1, nx)]

    def center(k, carry):
        part = pl.ds(pl.multiple_of(k * 64, 64), 64)
        zc_buf[part, :] = (z_buf[part, :].astype(F32) - mean).astype(BF16)
        return carry

    lax.fori_loop(0, local_rows // 64, center, 0, unroll=2)

    def transpose_columns(blocks):
        for k in blocks:
            zt_buf[pl.ds(k * 256, 256), :] = zc_buf[:, pl.ds(k * 256, 256)].T

    transpose_columns(range(HALF // 256))
    left, right = pl.ds(0, HALF), pl.ds(HALF, HALF)

    transpose_columns(range(HALF // 256, EXP // 256))
    row_at, col_at = iota((HALF, 256), 0), iota((HALF, 256), 1)
    for k in range(HALF // 256):
        in_left = mm(zt_buf[left, :], zc_buf[:, pl.ds(k * 256, 256)])
        in_right = mm(zt_buf[right, :], zc_buf[:, pl.ds(HALF + k * 256, 256)])
        ahead = col_at + k * 256 - row_at
        both = jnp.where(ahead > 0, in_left, jnp.where(ahead < 0, in_right, 0.0)).astype(BF16)
        for j in range(256 // lb):
            send_1[1, k * (256 // lb) + j] = both[:, j * lb : (j + 1) * lb]
    first_y = [
        remote(send_1.at[1, around(y, d, nx)], recv_1.at[1, d - 1], y_peers[d - 1])
        for d in range(1, nx)
    ]
    start(first_y)
    for k in range(HALF // 256):
        cols = pl.ds(HALF + k * 256, 256)
        cross = mm(zt_buf[left, :], zc_buf[:, cols]).astype(BF16)
        for j in range(256 // lb):
            send_1[0, k * (256 // lb) + j] = cross[:, j * lb : (j + 1) * lb]
    first_x = [
        remote(send_1.at[0, around(x, d, nx)], recv_1.at[0, d - 1], x_peers[d - 1])
        for d in range(1, nx)
    ]
    start(first_x)
    start(share_x)
    start(share_y)
    meanwhile("first")

    def combine(own, parts, n):
        center = own
        for i in range(n - 1):
            center = center + parts[i]
        center = center / n
        lines = [own - center] + [parts[i] - center for i in range(n - 1)]
        lines += [jnp.zeros_like(own)] * (8 - n)
        dev[...] = jnp.concatenate(lines, axis=0)
        return center

    def outer(first_at, height, second_at):
        return mm(
            dev[:, pl.ds(first_at, height)],
            dev[:, pl.ds(second_at, lb)],
            TN,
            precision=lax.Precision.HIGHEST,
        )

    def triangles(first_at, height, block_at, inner_at):
        in_left = outer(first_at, height, block_at)
        in_right = outer(HALF + first_at, height, HALF + block_at)
        ahead = (block_at + iota((height, lb), 1)) - (inner_at + iota((height, lb), 0))
        return jnp.where(ahead > 0, in_left, jnp.where(ahead < 0, in_right, 0.0))

    x_at, y_at = pl.multiple_of(x * lb, lb), pl.multiple_of(y * lb, lb)

    arrived(share_x)
    center_x = combine(mean0[0], mean_x, nx)
    mean1[0] = center_x
    carry_x = [remote(mean1.at[0], mean_x2.at[d - 1], y_peers[d - 1]) for d in range(1, nx)]
    start(carry_x)
    part = local_rows * outer(0, HALF, HALF + x_at)
    arrived(first_x)
    part = part + send_1[0, x].astype(F32)
    for i in range(nx - 1):
        part = part + recv_1[0, i].astype(F32)
    send_2[0] = part.astype(BF16)
    second_x = [
        remote(
            send_2.at[0, pl.ds(pl.multiple_of(around(y, d, nx) * lb, lb), lb)],
            recv_2.at[0, d - 1],
            y_peers[d - 1],
        )
        for d in range(1, nx)
    ]
    start(second_x)

    arrived(share_y)
    center_y = combine(mean0[0], mean_y, nx)
    mean1[1] = center_y
    carry_y = [remote(mean1.at[1], mean_y2.at[d - 1], x_peers[d - 1]) for d in range(1, nx)]
    start(carry_y)
    part = local_rows * triangles(0, HALF, y_at, 0)
    arrived(first_y)
    part = part + send_1[1, y].astype(F32)
    for i in range(nx - 1):
        part = part + recv_1[1, i].astype(F32)
    send_2[1] = part.astype(BF16)
    second_y = [
        remote(
            send_2.at[1, pl.ds(pl.multiple_of(around(x, d, nx) * lb, lb), lb)],
            recv_2.at[1, d - 1],
            x_peers[d - 1],
        )
        for d in range(1, nx)
    ]
    start(second_y)
    meanwhile("second")

    arrived(carry_x)
    center_xy = combine(mean1[0], mean_x2, nx)
    mean2[0] = center_xy
    carry_z = [remote(mean2.at[0], mean_z.at[d - 1], z_peers[d - 1]) for d in range(1, nz)]
    start(carry_z)
    part = (local_rows * nx) * outer(y_at, lb, HALF + x_at)
    arrived(second_x)
    part = part + send_2[0, pl.ds(y_at, lb)].astype(F32)
    for i in range(nx - 1):
        part = part + recv_2[0, i].astype(F32)
    send_3[0] = part.astype(BF16)

    arrived(carry_y)
    combine(mean1[1], mean_y2, nx)
    part = (local_rows * nx) * triangles(x_at, lb, y_at, x_at)
    arrived(second_y)
    part = part + send_2[1, pl.ds(x_at, lb)].astype(F32)
    for i in range(nx - 1):
        part = part + recv_2[1, i].astype(F32)
    send_3[1] = part.astype(BF16)

    def z_rows(i):
        return pl.ds(pl.multiple_of(i * zr, zr), zr)

    third = [
        remote(send_3.at[:, z_rows(around(z, d, nz))], recv_3.at[d - 1], z_peers[d - 1])
        for d in range(1, nz)
    ]
    start(third)
    meanwhile("third")
    arrived(carry_z)
    mean = combine(mean2[0], mean_z, nz)
    group_rows = local_rows * frames
    small[0] = group_rows * outer(y_at, lb, HALF + x_at)
    small[1] = group_rows * triangles(x_at, lb, y_at, x_at)
    arrived(third)
    part = small[:, z_rows(z), :] + send_3[:, z_rows(z), :].astype(F32)
    for i in range(nz - 1):
        part = part + recv_3[i].astype(F32)
    scale = 1.0 / (group_rows * nz - 1) / math.sqrt(EXP)
    cov_z[:, z_rows(z), :] = (part * scale).astype(BF16)

    back_z = [
        remote(cov_z.at[:, z_rows(z)], cov_z.at[:, z_rows(z)], z_peers[d - 1])
        for d in range(1, nz)
    ]
    start(back_z)

    def center_all(k, carry):
        part = pl.ds(pl.multiple_of(k * 64, 64), 64)
        zc_buf[part, :] = (z_buf[part, :].astype(F32) - mean).astype(BF16)
        return carry

    lax.fori_loop(0, local_rows // 64, center_all, 0)
    meanwhile("back z")
    arrived(back_z)
    y_rows, x_rows = pl.ds(y_at, lb), pl.ds(x_at, lb)
    back_2 = [
        remote(cov_z.at[0], cov_mid.at[0, y_rows], y_peers[d - 1]) for d in range(1, nx)
    ] + [remote(cov_z.at[1], cov_mid.at[1, x_rows], x_peers[d - 1]) for d in range(1, nx)]
    start(back_2)
    cov_mid[0, y_rows] = cov_z[0]
    cov_mid[1, x_rows] = cov_z[1]
    meanwhile("back 2")
    arrived(back_2)
    back_1 = [
        remote(cov_mid.at[0], cov_all.at[0, x], x_peers[d - 1]) for d in range(1, nx)
    ] + [remote(cov_mid.at[1], cov_all.at[1, y], y_peers[d - 1]) for d in range(1, nx)]
    start(back_1)
    cov_all[0, x] = cov_mid[0]
    cov_all[1, y] = cov_mid[1]

    meanwhile("back 1")

    pieces = HALF // lb
    arrived(back_1[: nx - 1])
    cross = jnp.concatenate([cov_all[0, k] for k in range(pieces)], axis=1)
    matrix[left, right] = cross
    matrix[right, left] = cross.T
    arrived(back_1[nx - 1 :])
    both = jnp.concatenate([cov_all[1, k] for k in range(pieces)], axis=1)
    turned = both.T
    ahead = iota((HALF, HALF), 1) - iota((HALF, HALF), 0)
    matrix[left, left] = jnp.where(ahead > 0, both, turned)
    matrix[right, right] = jnp.where(ahead < 0, both, turned)

    def gradient(slot, clip):
        lines = pl.ds(pl.multiple_of(clip * rows, rows), rows)
        for k in range(2):
            for j in range(2):
                cols = pl.ds(k * HALF + j * 256, 256)
                grads[slot, :, cols] = mm(zc_buf[lines, :], matrix[:, cols]).astype(BF16)
            cols = pl.ds(k * HALF, HALF)
            if slot == 0:
                copy = remote(grads.at[0, :, cols], grad_ref.at[core, :, cols], partner)
                start([copy])
            else:
                copy = pltpu.make_async_copy(
                    grads.at[1, :, cols], grad_ref.at[core, :, cols], local_sem.at[2 + k]
                )
                copy.start()
            results.append(copy)

    results = []
    gradient(0, other)
    gradient(1, core)

    arrived(strips)
    edge = STRIP - 256
    top, bottom = strip_recv[...], strip_own[...]
    flow_ref[:, 0:edge] = top[0:2, :edge]
    flow_ref[:, edge:STRIP] = top[0:2, edge:] + bottom[0:2, :256]
    flow_ref[:, STRIP:] = bottom[0:2, 256:]
    store = pltpu.make_async_copy(flow_ref, flow_any, local_sem.at[10])
    store.start()

    for copy in results:
        copy.wait_recv()
    store.wait()
    for c in range(PARTS):
        not_first(to_before[c].wait_send)
        not_last(to_after[c].wait_send)
    for copy in started:
        copy.wait_send()


def hand_out(flow_in, grads_in, flow_out, grads_out, flow_held, held, in_sem, out_sem):
    loads, stores = [], []
    for k in range(4):
        part = (k // 2, pl.ds((k % 2) * 128, 128))
        loads.append(pltpu.make_async_copy(grads_in.at[part], held.at[part], in_sem.at[k]))
        stores.append(pltpu.make_async_copy(held.at[part], grads_out.at[part], out_sem.at[k]))
    loads.append(pltpu.make_async_copy(flow_in, flow_held, in_sem.at[4]))
    stores.append(pltpu.make_async_copy(flow_held, flow_out, out_sem.at[4]))
    for load in loads:
        load.start()
    for load, store in zip(loads, stores):
        load.wait()
        store.start()
    for store in stores:
        store.wait()


def on_device(
    nx,
    nz,
    feat_a,
    feat_b,
    flow_in_weight,
    flow_entry_bias,
    flow_out_weight,
    frame_mix,
    expand_weight,
    expand_bias,
):
    frames = nx * nx
    block = POOLED // frames
    rows = frames * block
    lb = HALF // nx
    zr = lb // nz
    copies = 2 * frames - 1 + 2 * PARTS + 12 * (nx - 1) + 3 * (nz - 1) + 3
    hbm = pl.BlockSpec(memory_space=pl.ANY)
    scratch = [
        pltpu.VMEM((DISP, DEC), F32),
        pltpu.VMEM((1, DEC), F32),
        pltpu.VMEM((3, 3, 2, DEC), F32),
        pltpu.VMEM((frames, frames), F32),
        pltpu.VMEM((D_FEAT, EXP), BF16),
        pltpu.VMEM((1, EXP), F32),
        pltpu.VMEM((2, POSITIONS), F32),
        pltpu.VMEM((REACH + POSITIONS, D_FEAT), BF16),
        pltpu.VMEM((POSITIONS, D_FEAT), BF16),
        pltpu.VMEM((POSITIONS, D_FEAT), BF16),
        pltpu.VMEM((NEXT_ROWS, D_FEAT), BF16),
        pltpu.VMEM((TASK, D_FEAT), BF16),
        pltpu.VMEM((2, 640, DEC), BF16),
        pltpu.VMEM((32, DEC), BF16),
        pltpu.VMEM((2, rows, rows), BF16),
        pltpu.VMEM((frames, 2, block, D_FEAT), BF16),
        pltpu.VMEM((2, frames, block, D_FEAT), BF16),
        pltpu.VMEM((2 * rows, EXP), BF16),
        pltpu.VMEM((2 * rows, EXP), BF16),
        pltpu.VMEM((EXP, 2 * rows), BF16),
        pltpu.VMEM((1, 1, EXP), F32),
        pltpu.VMEM((nx - 1, 1, EXP), F32),
        pltpu.VMEM((nx - 1, 1, EXP), F32),
        pltpu.VMEM((2, 1, EXP), F32),
        pltpu.VMEM((nx - 1, 1, EXP), F32),
        pltpu.VMEM((nx - 1, 1, EXP), F32),
        pltpu.VMEM((1, 1, EXP), F32),
        pltpu.VMEM((nz - 1, 1, EXP), F32),
        pltpu.VMEM((8, EXP), F32),
        pltpu.VMEM((2, nx, HALF, lb), BF16),
        pltpu.VMEM((2, nx - 1, HALF, lb), BF16),
        pltpu.VMEM((2, HALF, lb), BF16),
        pltpu.VMEM((2, nx - 1, lb, lb), BF16),
        pltpu.VMEM((2, lb, lb), BF16),
        pltpu.VMEM((nz - 1, 2, zr, lb), BF16),
        pltpu.VMEM((2, lb, lb), F32),
        pltpu.VMEM((2, lb, lb), BF16),
        pltpu.VMEM((2, HALF, lb), BF16),
        pltpu.VMEM((2, nx, HALF, lb), BF16),
        pltpu.VMEM((EXP, EXP), BF16),
        pltpu.VMEM((2, TASK, DEC), BF16),
        pltpu.VMEM((8, STRIP), F32),
        pltpu.VMEM((8, STRIP), F32),
        pltpu.VMEM((8, STRIP), F32),
        pltpu.VMEM((2, rows, EXP), BF16),
        pltpu.SemaphoreType.DMA((11,)),
        pltpu.SemaphoreType.DMA((8,)),
        pltpu.SemaphoreType.DMA((copies,)),
        pltpu.SemaphoreType.DMA((copies,)),
    ]
    flow, grads = pl.pallas_call(
        functools.partial(kernel, nx, nz),
        out_shape=[
            jax.ShapeDtypeStruct((2, POSITIONS), F32),
            jax.ShapeDtypeStruct((2, rows, EXP), BF16),
        ],
        in_specs=[hbm] * 8,
        out_specs=[hbm, hbm],
        scratch_shapes=scratch,
        compiler_params=pltpu.CompilerParams(
            collective_id=0, has_side_effects=True, vmem_limit_bytes=56 * 1024 * 1024
        ),
    )(
        feat_a,
        feat_b,
        flow_in_weight.T,
        flow_entry_bias.reshape(1, DEC),
        flow_out_weight,
        frame_mix,
        expand_weight,
        expand_bias.reshape(1, EXP),
    )
    flow, grads = pl.pallas_call(
        hand_out,
        out_shape=[
            jax.ShapeDtypeStruct((2, POSITIONS), F32),
            jax.ShapeDtypeStruct((2, rows, EXP), BF16),
        ],
        in_specs=[hbm, hbm],
        out_specs=[hbm, hbm],
        scratch_shapes=[
            pltpu.VMEM((2, POSITIONS), F32),
            pltpu.VMEM((2, rows, EXP), BF16),
            pltpu.SemaphoreType.DMA((5,)),
            pltpu.SemaphoreType.DMA((5,)),
        ],
    )(flow, grads)
    return (
        flow.reshape(1, 1, 2, POSITIONS),
        grads.reshape(2, 1, frames, block, EXP),
    )


def solution(mesh):
    nx = math.isqrt(mesh.shape["tm"])
    nz = mesh.shape["batch"] // 2
    return jax.shard_map(
        functools.partial(on_device, nx, nz),
        mesh=mesh,
        in_specs=(
            P("batch", "tm", None, None),
            P("batch", "tm", None, None),
            P(),
            P(),
            P(),
            P(),
            P(),
            P(),
        ),
        out_specs=(P("batch", "tm", None, None), P(None, "batch", None, "tm", None)),
        check_vma=False,
    )
```

```python
import functools
import math

import jax
import jax.numpy as jnp
from jax import lax
from jax.experimental import pallas as pl
from jax.experimental.pallas import tpu as pltpu
from jax.sharding import PartitionSpec as P

MESH = pl.DeviceIdType.MESH
F32 = jnp.float32
BF16 = jnp.bfloat16

HF = 64
WF = 64
D_FEAT = 256
EXP = 1024
HALF = EXP // 2
DEC = 128
DISP = 81
POSITIONS = HF * WF
POOLED = 256
GROUP = 4 * WF
TASK = 32 * WF
REACH = 4 * WF
NEXT_ROWS = TASK + 2 * REACH
UNROLL = 2
PARTS = 4
STRIP = 34 * WF

SCHEDULE = {
    "embed": [("send", 0, 1)],
    "first": [("send", 1, 2)],
    "second": [("send", 2, 3)],
    "third": [("send", 3, 4), ("upper", 0, 2)],
    "back z": [("upper", 2, 4), ("lower", 0, 2)],
    "back 2": [("upper", 4, 6), ("lower", 2, 4)],
    "back 1": [("upper", 6, 8), ("lower", 4, 8)],
}

NN = (((1,), (0,)), ((), ()))
NT = (((1,), (1,)), ((), ()))
TN = (((0,), (0,)), ((), ()))


def mm(a, b, dims=NN, precision=None):
    return lax.dot_general(a, b, dims, precision=precision, preferred_element_type=F32)


def iota(shape, axis):
    return lax.broadcasted_iota(jnp.int32, shape, axis)


def gelu(x):
    return 0.5 * x * (1.0 + jnp.tanh(math.sqrt(2.0 / math.pi) * (x + 0.044715 * (x * x * x))))


def one_hot(condition):
    return jnp.where(condition, 1.0, 0.0).astype(BF16)


def turn(size, kind):
    hit = (iota((size, size), 0) ^ 63) == iota((size, size), 1)
    return jnp.where(hit, 1.0, 0.0).astype(kind)


def band_weights(w_in, odd):
    shape = (5 * 128, DISP)
    row, col = iota(shape, 0), iota(shape, 1)
    lane = (row + 4) & 127
    dy = (row >> 7) * 2 + 1 - (lane >> 6) - odd
    dx = lane & 63
    hit = (dx < 9) & (dy >= 0) & (dy < 9) & (dy * 9 + dx == col)
    return (mm(one_hot(hit), w_in.astype(BF16)) * (1.0 / math.sqrt(D_FEAT))).astype(BF16)


def conv_weights(w_out_ref):
    zeros = jnp.zeros((2, DEC), F32)
    rows = []
    for kx in (2, 1, 0):
        rows += [w_out_ref[ky, kx] for ky in range(3)] + [zeros]
    rows += [jnp.zeros((8, DEC), F32)]
    return jnp.concatenate(rows, axis=0).astype(BF16)


def mixing_weights(mix, frames, block):
    size = frames * block
    spread = one_hot(lax.div(iota((size, frames), 0), block) == iota((size, frames), 1))
    same = lax.rem(iota((size, size), 0), block) == lax.rem(iota((size, size), 1), block)
    high = mix.astype(BF16)
    low = (mix - high.astype(F32)).astype(BF16)
    parts = []
    for part in (high, low):
        rows = mm(spread, part).astype(BF16)
        parts.append(jnp.where(same, mm(rows, spread, NT), 0.0).astype(BF16))
    return parts


def hidden_rows(low, high, first_ref, first_at, next_ref, next_at, band_ref, bias, hid_ref):
    x, lane = 63 - iota((WF, 128), 0), (iota((WF, 128), 1) + 4) & 63
    inside = (lane < 9) & (x + lane >= 4) & (x + lane < WF + 4)

    def group(g, carry):
        at = pl.multiple_of(g * GROUP, GROUP)
        first = first_ref[pl.ds(first_at + at, GROUP), :]
        latter = next_ref[pl.ds(next_at + at, 3 * GROUP), :]
        products = mm(first, latter, NT)
        for odd in range(2):
            pieces = []
            for i in (odd, odd + 2):
                blocks = []
                for m in range(i // 2, i // 2 + 5):
                    block = products[i * WF : (i + 1) * WF, m * 128 : (m + 1) * 128]
                    block = pltpu.roll(block, 1, 1, stride=1, stride_axis=0)
                    blocks.append(jnp.where(inside, block, 0.0).astype(BF16))
                pieces.append(jnp.concatenate(blocks, axis=1))
            skewed = jnp.concatenate(pieces, axis=0)
            hidden = gelu(mm(skewed, band_ref[odd]) + bias).astype(BF16)
            hid_ref[pl.ds(at + odd * WF, WF), :] = hidden[:WF]
            hid_ref[pl.ds(at + (odd + 2) * WF, WF), :] = hidden[WF:]
        return carry

    lax.fori_loop(low, high, group, 0, unroll=UNROLL)


def flow_rows(hid_ref, conv, base):
    taps = mm(conv, hid_ref[...], NT)
    lane = iota((8, TASK), 1) & 63
    across = (
        taps[8:16]
        + jnp.where(lane != 0, pltpu.roll(taps[0:8], 1, 1), 0.0)
        + jnp.where(lane != 63, pltpu.roll(taps[16:24], TASK - 1, 1), 0.0)
    )
    wide = TASK + 256
    across = jnp.concatenate([across, jnp.zeros((8, 256), F32)], axis=1)
    total = pltpu.roll(across, base + 64, 1)
    middle = pltpu.roll(across, base, 1) if base else across
    total = total + pltpu.roll(middle, 6, 0)
    total = total + pltpu.roll(pltpu.roll(across, (base + wide - 64) % wide, 1), 4, 0)
    blocks = [total[:, k * 128 : (k + 1) * 128] for k in range(STRIP // 128)]
    turned = mm(jnp.concatenate(blocks, axis=0), turn(128, F32), precision=lax.Precision.HIGHEST)
    return jnp.concatenate([turned[k * 8 : (k + 1) * 8] for k in range(STRIP // 128)], axis=1)


def kernel(
    nx,
    nz,
    fa_ref,
    fb_ref,
    w_in_any,
    b_in_any,
    w_out_any,
    mix_any,
    ew_any,
    eb_any,
    flow_any,
    grad_ref,
    w_in_ref,
    b_in_ref,
    w_out_ref,
    mix_ref,
    ew_ref,
    eb_ref,
    flow_ref,
    a_buf,
    b_buf,
    t_buf,
    rn_buf,
    rp_buf,
    band,
    conv,
    mixer,
    pooled,
    got,
    z_buf,
    zc_buf,
    zt_buf,
    mean0,
    mean_x,
    mean_y,
    mean1,
    mean_x2,
    mean_y2,
    mean2,
    mean_z,
    dev,
    send_1,
    recv_1,
    send_2,
    recv_2,
    send_3,
    recv_3,
    small,
    cov_z,
    cov_mid,
    cov_all,
    matrix,
    hid,
    strip_send,
    strip_recv,
    strip_own,
    grads,
    local_sem,
    view_sem,
    send_sem,
    recv_sem,
):
    frames = nx * nx
    block = POOLED // frames
    rows = frames * block
    local_rows = 2 * rows
    lb = HALF // nx
    zr = lb // nz

    batch, t = lax.axis_index("batch"), lax.axis_index("tm")
    z, core = lax.div(batch, 2), lax.rem(batch, 2)
    x, y = lax.div(t, nx), lax.rem(t, nx)
    other = 1 - core

    def around(i, d, n):
        return lax.rem(i + d, n)

    x_peers = [(batch, around(x, d, nx) * nx + y) for d in range(1, nx)]
    y_peers = [(batch, x * nx + around(y, d, nx)) for d in range(1, nx)]
    z_peers = [(around(z, d, nz) * 2 + core, t) for d in range(1, nz)]
    partner = (z * 2 + other, t)
    before = (batch, lax.rem(t + frames - 1, frames))
    after = (batch, lax.rem(t + 1, frames))

    count = [0]

    def remote(src, dst, device):
        i = count[0]
        count[0] += 1
        return pltpu.make_async_remote_copy(
            src_ref=src,
            dst_ref=dst,
            send_sem=send_sem.at[i],
            recv_sem=recv_sem.at[i],
            device_id=device,
            device_id_type=MESH,
        )

    def start(copies):
        for copy in copies:
            copy.start()
        started.extend(copies)

    def arrived(copies):
        for copy in copies:
            copy.wait_recv()

    started = []

    quarter = POSITIONS // 4
    load_views = []
    for k in range(4):
        part = pl.ds(k * quarter, quarter)
        load_views += [
            pltpu.make_async_copy(
                fa_ref.at[0, 0, part], a_buf.at[pl.ds(REACH + k * quarter, quarter)], view_sem.at[k]
            ),
            pltpu.make_async_copy(fb_ref.at[0, 0, part], b_buf.at[part], view_sem.at[4 + k]),
        ]
    load_mix = pltpu.make_async_copy(mix_any, mix_ref, local_sem.at[4])
    load_mix.start()
    for load in load_views:
        load.start()
    loads = []
    for i, (source, target) in enumerate(
        [(w_in_any, w_in_ref), (b_in_any, b_in_ref), (w_out_any, w_out_ref), (ew_any, ew_ref), (eb_any, eb_ref)]
    ):
        loads.append(pltpu.make_async_copy(source, target, local_sem.at[5 + i]))
        loads[i].start()

    barrier = pltpu.get_barrier_semaphore()
    for device in z_peers + [partner]:
        pl.semaphore_signal(barrier, inc=1, device_id=device, device_id_type=MESH)

    def greet(d, carry):
        for c in range(2):
            device = (z * 2 + c, around(t, d, frames))
            pl.semaphore_signal(barrier, inc=1, device_id=device, device_id_type=MESH)
        return carry

    lax.fori_loop(1, frames, greet, 0)
    span = POSITIONS // frames
    prow, pcol = iota((block, span), 0), iota((block, span), 1)
    pooled_at = lax.div(pcol, GROUP) * 16 + lax.div(pcol & 63, 4)
    pool = one_hot(pooled_at == prow)

    def pool_block(k, carry):
        at = pl.multiple_of(k * span, span)
        from_a = mm(pool, a_buf[pl.ds(REACH + at, span), :]) * (1.0 / 16.0)
        pooled[k, 0] = from_a.astype(BF16)
        from_b = mm(pool, b_buf[pl.ds(at, span), :]) * (1.0 / 16.0)
        pooled[k, 1] = from_b.astype(BF16)
        return carry

    for k in range(4):
        load_views[2 * k].wait()
        load_views[2 * k + 1].wait()
        lax.fori_loop(k * frames // 4, (k + 1) * frames // 4, pool_block, 0, unroll=True)
    pl.semaphore_wait(barrier, nz - 1 + 1 + 2 * (frames - 1))

    exchange = []
    for d in range(frames):
        to = around(t, d, frames)
        for view, device in ((core, (batch, to)), (other, (z * 2 + other, to))):
            if d > 0 or view is other:
                exchange.append(remote(pooled.at[to, view], got.at[core, t], device))
    start(exchange)

    turner = turn(GROUP, BF16)

    def turn_group(k, carry):
        at = pl.multiple_of(k * GROUP, GROUP)
        turned = mm(turner, a_buf[pl.ds(REACH + at, GROUP), :])
        t_buf[pl.ds(at, GROUP), :] = turned.astype(BF16)
        return carry

    lax.fori_loop(0, TASK // GROUP, turn_group, 0, unroll=4)

    to_after, to_before = [], []
    for c in range(PARTS):
        at, size = c * 8 * WF, 8 * WF
        to_after.append(remote(t_buf.at[pl.ds(at, size)], rp_buf.at[pl.ds(at, size)], after))
        at, size = c * 8 * WF, (12 if c == PARTS - 1 else 8) * WF
        to_before.append(remote(a_buf.at[pl.ds(TASK + at, size)], rn_buf.at[pl.ds(at, size)], before))

    def not_first(action):
        pl.when(t > 0)(action)

    def not_last(action):
        pl.when(t < frames - 1)(action)

    ready = set()
    strips = []

    def await_part(view, c):
        if (view, c) not in ready:
            ready.add((view, c))
            if view == 0:
                not_first(to_after[c].wait_recv)
            else:
                not_last(to_before[c].wait_recv)

    def meanwhile(point):
        for kind, low, high in SCHEDULE.get(point, ()):
            if kind == "send":
                for c in range(low, high):
                    not_first(to_before[c].start)
                    not_last(to_after[c].start)
            elif kind == "upper":
                for c in range((high + 1) // 2):
                    await_part(0, c)
                hidden_rows(low, high, rp_buf, 0, a_buf, 0, band, bias, hid.at[0])
                if high == TASK // GROUP:
                    strip_send[...] = flow_rows(hid.at[0], conv[...], 0)
                    strips.append(remote(strip_send, strip_recv, before))
                    start(strips)
            else:
                for c in range(min(PARTS, (high + 3) // 2)):
                    await_part(1, c)
                hidden_rows(low, high, t_buf, TASK, rn_buf, 0, band, bias, hid.at[1])
                if high == TASK // GROUP:
                    strip_own[...] = flow_rows(hid.at[1], conv[...], 128)

    a_buf[pl.ds(0, REACH), :] = jnp.zeros((REACH, D_FEAT), BF16)
    rn_buf[pl.ds(TASK + REACH, REACH), :] = jnp.zeros((REACH, D_FEAT), BF16)

    @pl.when(t == frames - 1)
    def _():
        rn_buf[pl.ds(0, TASK + REACH), :] = jnp.zeros((TASK + REACH, D_FEAT), BF16)

    @pl.when(t == 0)
    def _():
        rp_buf[...] = jnp.zeros((TASK, D_FEAT), BF16)

    meanwhile("exchange")
    got[core, t] = pooled[t, core]
    load_mix.wait()
    for load in loads:
        load.wait()
    bias = b_in_ref[...]
    mixer[0], mixer[1] = mixing_weights(mix_ref[...], frames, block)
    lax.fori_loop(TASK // GROUP, 2 * (TASK // GROUP), turn_group, 0, unroll=4)
    band[0] = band_weights(w_in_ref[...], 0)
    band[1] = band_weights(w_in_ref[...], 1)
    conv[...] = conv_weights(w_out_ref)
    arrived(exchange)
    meanwhile("embed")

    total = [jnp.zeros((1, 256), F32) for _ in range(EXP // 256)]
    for clip in range(2):
        features = got[clip].reshape(rows, D_FEAT)
        mixed = (mm(mixer[0], features) + mm(mixer[1], features)).astype(BF16)
        for k in range(EXP // 256):
            cols = pl.ds(k * 256, 256)
            value = gelu(mm(mixed, ew_ref[:, cols]) + eb_ref[:, cols]).astype(BF16)
            z_buf[pl.ds(clip * rows, rows), cols] = value
            total[k] = total[k] + jnp.sum(value.astype(F32), axis=0, keepdims=True)
    mean = jnp.concatenate(total, axis=1) / local_rows
    mean0[0] = mean
    share_x = [remote(mean0.at[0], mean_x.at[d - 1], x_peers[d - 1]) for d in range(1, nx)]
    share_y = [remote(mean0.at[0], mean_y.at[d - 1], y_peers[d - 1]) for d in range(1, nx)]

    def center(k, carry):
        part = pl.ds(pl.multiple_of(k * 64, 64), 64)
        zc_buf[part, :] = (z_buf[part, :].astype(F32) - mean).astype(BF16)
        return carry

    lax.fori_loop(0, local_rows // 64, center, 0, unroll=2)

    def transpose_columns(blocks):
        for k in blocks:
            zt_buf[pl.ds(k * 256, 256), :] = zc_buf[:, pl.ds(k * 256, 256)].T

    transpose_columns(range(HALF // 256))
    left, right = pl.ds(0, HALF), pl.ds(HALF, HALF)

    transpose_columns(range(HALF // 256, EXP // 256))
    row_at, col_at = iota((HALF, 256), 0), iota((HALF, 256), 1)
    for k in range(HALF // 256):
        in_left = mm(zt_buf[left, :], zc_buf[:, pl.ds(k * 256, 256)])
        in_right = mm(zt_buf[right, :], zc_buf[:, pl.ds(HALF + k * 256, 256)])
        ahead = col_at + k * 256 - row_at
        both = jnp.where(ahead > 0, in_left, jnp.where(ahead < 0, in_right, 0.0)).astype(BF16)
        for j in range(256 // lb):
            send_1[1, k * (256 // lb) + j] = both[:, j * lb : (j + 1) * lb]
    first_y = [
        remote(send_1.at[1, around(y, d, nx)], recv_1.at[1, d - 1], y_peers[d - 1])
        for d in range(1, nx)
    ]
    start(first_y)
    for k in range(HALF // 256):
        cols = pl.ds(HALF + k * 256, 256)
        cross = mm(zt_buf[left, :], zc_buf[:, cols]).astype(BF16)
        for j in range(256 // lb):
            send_1[0, k * (256 // lb) + j] = cross[:, j * lb : (j + 1) * lb]
    first_x = [
        remote(send_1.at[0, around(x, d, nx)], recv_1.at[0, d - 1], x_peers[d - 1])
        for d in range(1, nx)
    ]
    start(first_x)
    start(share_x)
    start(share_y)
    meanwhile("first")

    def combine(own, parts, n):
        center = own
        for i in range(n - 1):
            center = center + parts[i]
        center = center / n
        lines = [own - center] + [parts[i] - center for i in range(n - 1)]
        lines += [jnp.zeros_like(own)] * (8 - n)
        dev[...] = jnp.concatenate(lines, axis=0)
        return center

    def outer(first_at, height, second_at):
        return mm(
            dev[:, pl.ds(first_at, height)],
            dev[:, pl.ds(second_at, lb)],
            TN,
            precision=lax.Precision.HIGHEST,
        )

    def triangles(first_at, height, block_at, inner_at):
        in_left = outer(first_at, height, block_at)
        in_right = outer(HALF + first_at, height, HALF + block_at)
        ahead = (block_at + iota((height, lb), 1)) - (inner_at + iota((height, lb), 0))
        return jnp.where(ahead > 0, in_left, jnp.where(ahead < 0, in_right, 0.0))

    x_at, y_at = pl.multiple_of(x * lb, lb), pl.multiple_of(y * lb, lb)

    arrived(share_x)
    center_x = combine(mean0[0], mean_x, nx)
    mean1[0] = center_x
    carry_x = [remote(mean1.at[0], mean_x2.at[d - 1], y_peers[d - 1]) for d in range(1, nx)]
    start(carry_x)
    part = local_rows * outer(0, HALF, HALF + x_at)
    arrived(first_x)
    part = part + send_1[0, x].astype(F32)
    for i in range(nx - 1):
        part = part + recv_1[0, i].astype(F32)
    send_2[0] = part.astype(BF16)
    second_x = [
        remote(
            send_2.at[0, pl.ds(pl.multiple_of(around(y, d, nx) * lb, lb), lb)],
            recv_2.at[0, d - 1],
            y_peers[d - 1],
        )
        for d in range(1, nx)
    ]
    start(second_x)

    arrived(share_y)
    center_y = combine(mean0[0], mean_y, nx)
    mean1[1] = center_y
    carry_y = [remote(mean1.at[1], mean_y2.at[d - 1], x_peers[d - 1]) for d in range(1, nx)]
    start(carry_y)
    part = local_rows * triangles(0, HALF, y_at, 0)
    arrived(first_y)
    part = part + send_1[1, y].astype(F32)
    for i in range(nx - 1):
        part = part + recv_1[1, i].astype(F32)
    send_2[1] = part.astype(BF16)
    second_y = [
        remote(
            send_2.at[1, pl.ds(pl.multiple_of(around(x, d, nx) * lb, lb), lb)],
            recv_2.at[1, d - 1],
            x_peers[d - 1],
        )
        for d in range(1, nx)
    ]
    start(second_y)
    meanwhile("second")

    arrived(carry_x)
    center_xy = combine(mean1[0], mean_x2, nx)
    mean2[0] = center_xy
    carry_z = [remote(mean2.at[0], mean_z.at[d - 1], z_peers[d - 1]) for d in range(1, nz)]
    start(carry_z)
    part = (local_rows * nx) * outer(y_at, lb, HALF + x_at)
    arrived(second_x)
    part = part + send_2[0, pl.ds(y_at, lb)].astype(F32)
    for i in range(nx - 1):
        part = part + recv_2[0, i].astype(F32)
    send_3[0] = part.astype(BF16)

    arrived(carry_y)
    combine(mean1[1], mean_y2, nx)
    part = (local_rows * nx) * triangles(x_at, lb, y_at, x_at)
    arrived(second_y)
    part = part + send_2[1, pl.ds(x_at, lb)].astype(F32)
    for i in range(nx - 1):
        part = part + recv_2[1, i].astype(F32)
    send_3[1] = part.astype(BF16)

    def z_rows(i):
        return pl.ds(pl.multiple_of(i * zr, zr), zr)

    third = [
        remote(send_3.at[:, z_rows(around(z, d, nz))], recv_3.at[d - 1], z_peers[d - 1])
        for d in range(1, nz)
    ]
    start(third)
    meanwhile("third")
    arrived(carry_z)
    mean = combine(mean2[0], mean_z, nz)
    group_rows = local_rows * frames
    small[0] = group_rows * outer(y_at, lb, HALF + x_at)
    small[1] = group_rows * triangles(x_at, lb, y_at, x_at)
    arrived(third)
    part = small[:, z_rows(z), :] + send_3[:, z_rows(z), :].astype(F32)
    for i in range(nz - 1):
        part = part + recv_3[i].astype(F32)
    scale = 1.0 / (group_rows * nz - 1) / math.sqrt(EXP)
    cov_z[:, z_rows(z), :] = (part * scale).astype(BF16)

    back_z = [
        remote(cov_z.at[:, z_rows(z)], cov_z.at[:, z_rows(z)], z_peers[d - 1])
        for d in range(1, nz)
    ]
    start(back_z)

    def center_all(k, carry):
        part = pl.ds(pl.multiple_of(k * 64, 64), 64)
        zc_buf[part, :] = (z_buf[part, :].astype(F32) - mean).astype(BF16)
        return carry

    lax.fori_loop(0, local_rows // 64, center_all, 0)
    meanwhile("back z")
    arrived(back_z)
    y_rows, x_rows = pl.ds(y_at, lb), pl.ds(x_at, lb)
    back_2 = [
        remote(cov_z.at[0], cov_mid.at[0, y_rows], y_peers[d - 1]) for d in range(1, nx)
    ] + [remote(cov_z.at[1], cov_mid.at[1, x_rows], x_peers[d - 1]) for d in range(1, nx)]
    start(back_2)
    cov_mid[0, y_rows] = cov_z[0]
    cov_mid[1, x_rows] = cov_z[1]
    meanwhile("back 2")
    arrived(back_2)
    back_1 = [
        remote(cov_mid.at[0], cov_all.at[0, x], x_peers[d - 1]) for d in range(1, nx)
    ] + [remote(cov_mid.at[1], cov_all.at[1, y], y_peers[d - 1]) for d in range(1, nx)]
    start(back_1)
    cov_all[0, x] = cov_mid[0]
    cov_all[1, y] = cov_mid[1]

    meanwhile("back 1")

    pieces = HALF // lb
    arrived(back_1[: nx - 1])
    cross = jnp.concatenate([cov_all[0, k] for k in range(pieces)], axis=1)
    matrix[left, right] = cross
    matrix[right, left] = cross.T
    arrived(back_1[nx - 1 :])
    both = jnp.concatenate([cov_all[1, k] for k in range(pieces)], axis=1)
    turned = both.T
    ahead = iota((HALF, HALF), 1) - iota((HALF, HALF), 0)
    matrix[left, left] = jnp.where(ahead > 0, both, turned)
    matrix[right, right] = jnp.where(ahead < 0, both, turned)

    def gradient(slot, clip):
        lines = pl.ds(pl.multiple_of(clip * rows, rows), rows)
        for k in range(4):
            cols = pl.ds(k * 256, 256)
            grads[slot, :, cols] = mm(zc_buf[lines, :], matrix[:, cols]).astype(BF16)
            if slot == 0:
                copy = remote(grads.at[0, :, cols], grad_ref.at[core, :, cols], partner)
                start([copy])
            else:
                copy = pltpu.make_async_copy(
                    grads.at[1, :, cols], grad_ref.at[core, :, cols], local_sem.at[(0, 1, 2, 3)[k]]
                )
                copy.start()
            results.append(copy)

    results = []
    gradient(0, other)
    gradient(1, core)

    arrived(strips)
    edge = STRIP - 256
    top, bottom = strip_recv[...], strip_own[...]
    flow_ref[:, 0:edge] = top[0:2, :edge]
    flow_ref[:, edge:STRIP] = top[0:2, edge:] + bottom[0:2, :256]
    flow_ref[:, STRIP:] = bottom[0:2, 256:]
    store = pltpu.make_async_copy(flow_ref, flow_any, local_sem.at[10])
    store.start()

    for copy in results:
        copy.wait_recv()
    store.wait()
    for c in range(PARTS):
        not_first(to_before[c].wait_send)
        not_last(to_after[c].wait_send)
    for copy in started:
        copy.wait_send()


def hand_out(flow_in, grads_in, flow_out, grads_out, flow_held, held, in_sem, out_sem):
    loads, stores = [], []
    for k in range(4):
        part = (k // 2, pl.ds((k % 2) * 128, 128))
        loads.append(pltpu.make_async_copy(grads_in.at[part], held.at[part], in_sem.at[k]))
        stores.append(pltpu.make_async_copy(held.at[part], grads_out.at[part], out_sem.at[k]))
    loads.append(pltpu.make_async_copy(flow_in, flow_held, in_sem.at[4]))
    stores.append(pltpu.make_async_copy(flow_held, flow_out, out_sem.at[4]))
    for load in loads:
        load.start()
    for load, store in zip(loads, stores):
        load.wait()
        store.start()
    for store in stores:
        store.wait()


def on_device(
    nx,
    nz,
    feat_a,
    feat_b,
    flow_in_weight,
    flow_entry_bias,
    flow_out_weight,
    frame_mix,
    expand_weight,
    expand_bias,
):
    frames = nx * nx
    block = POOLED // frames
    rows = frames * block
    lb = HALF // nx
    zr = lb // nz
    copies = 2 * frames - 1 + 2 * PARTS + 12 * (nx - 1) + 3 * (nz - 1) + 5
    hbm = pl.BlockSpec(memory_space=pl.ANY)
    scratch = [
        pltpu.VMEM((DISP, DEC), F32),
        pltpu.VMEM((1, DEC), F32),
        pltpu.VMEM((3, 3, 2, DEC), F32),
        pltpu.VMEM((frames, frames), F32),
        pltpu.VMEM((D_FEAT, EXP), BF16),
        pltpu.VMEM((1, EXP), F32),
        pltpu.VMEM((2, POSITIONS), F32),
        pltpu.VMEM((REACH + POSITIONS, D_FEAT), BF16),
        pltpu.VMEM((POSITIONS, D_FEAT), BF16),
        pltpu.VMEM((POSITIONS, D_FEAT), BF16),
        pltpu.VMEM((NEXT_ROWS, D_FEAT), BF16),
        pltpu.VMEM((TASK, D_FEAT), BF16),
        pltpu.VMEM((2, 640, DEC), BF16),
        pltpu.VMEM((32, DEC), BF16),
        pltpu.VMEM((2, rows, rows), BF16),
        pltpu.VMEM((frames, 2, block, D_FEAT), BF16),
        pltpu.VMEM((2, frames, block, D_FEAT), BF16),
        pltpu.VMEM((2 * rows, EXP), BF16),
        pltpu.VMEM((2 * rows, EXP), BF16),
        pltpu.VMEM((EXP, 2 * rows), BF16),
        pltpu.VMEM((1, 1, EXP), F32),
        pltpu.VMEM((nx - 1, 1, EXP), F32),
        pltpu.VMEM((nx - 1, 1, EXP), F32),
        pltpu.VMEM((2, 1, EXP), F32),
        pltpu.VMEM((nx - 1, 1, EXP), F32),
        pltpu.VMEM((nx - 1, 1, EXP), F32),
        pltpu.VMEM((1, 1, EXP), F32),
        pltpu.VMEM((nz - 1, 1, EXP), F32),
        pltpu.VMEM((8, EXP), F32),
        pltpu.VMEM((2, nx, HALF, lb), BF16),
        pltpu.VMEM((2, nx - 1, HALF, lb), BF16),
        pltpu.VMEM((2, HALF, lb), BF16),
        pltpu.VMEM((2, nx - 1, lb, lb), BF16),
        pltpu.VMEM((2, lb, lb), BF16),
        pltpu.VMEM((nz - 1, 2, zr, lb), BF16),
        pltpu.VMEM((2, lb, lb), F32),
        pltpu.VMEM((2, lb, lb), BF16),
        pltpu.VMEM((2, HALF, lb), BF16),
        pltpu.VMEM((2, nx, HALF, lb), BF16),
        pltpu.VMEM((EXP, EXP), BF16),
        pltpu.VMEM((2, TASK, DEC), BF16),
        pltpu.VMEM((8, STRIP), F32),
        pltpu.VMEM((8, STRIP), F32),
        pltpu.VMEM((8, STRIP), F32),
        pltpu.VMEM((2, rows, EXP), BF16),
        pltpu.SemaphoreType.DMA((11,)),
        pltpu.SemaphoreType.DMA((8,)),
        pltpu.SemaphoreType.DMA((copies,)),
        pltpu.SemaphoreType.DMA((copies,)),
    ]
    flow, grads = pl.pallas_call(
        functools.partial(kernel, nx, nz),
        out_shape=[
            jax.ShapeDtypeStruct((2, POSITIONS), F32),
            jax.ShapeDtypeStruct((2, rows, EXP), BF16),
        ],
        in_specs=[hbm] * 8,
        out_specs=[hbm, hbm],
        scratch_shapes=scratch,
        compiler_params=pltpu.CompilerParams(
            collective_id=0, has_side_effects=True, vmem_limit_bytes=56 * 1024 * 1024
        ),
    )(
        feat_a,
        feat_b,
        flow_in_weight.T,
        flow_entry_bias.reshape(1, DEC),
        flow_out_weight,
        frame_mix,
        expand_weight,
        expand_bias.reshape(1, EXP),
    )
    flow, grads = pl.pallas_call(
        hand_out,
        out_shape=[
            jax.ShapeDtypeStruct((2, POSITIONS), F32),
            jax.ShapeDtypeStruct((2, rows, EXP), BF16),
        ],
        in_specs=[hbm, hbm],
        out_specs=[hbm, hbm],
        scratch_shapes=[
            pltpu.VMEM((2, POSITIONS), F32),
            pltpu.VMEM((2, rows, EXP), BF16),
            pltpu.SemaphoreType.DMA((5,)),
            pltpu.SemaphoreType.DMA((5,)),
        ],
    )(flow, grads)
    return (
        flow.reshape(1, 1, 2, POSITIONS),
        grads.reshape(2, 1, frames, block, EXP),
    )


def solution(mesh):
    nx = math.isqrt(mesh.shape["tm"])
    nz = mesh.shape["batch"] // 2
    return jax.shard_map(
        functools.partial(on_device, nx, nz),
        mesh=mesh,
        in_specs=(
            P("batch", "tm", None, None),
            P("batch", "tm", None, None),
            P(),
            P(),
            P(),
            P(),
            P(),
            P(),
        ),
        out_specs=(P("batch", "tm", None, None), P(None, "batch", None, "tm", None)),
        check_vma=False,
    )
```
